32 devices in a mesh: dp: 16 (over z, x, core), src: 2 (over y).
Axes of the slice: x: 2, y: 2, z: 4, core: 2. Of those that a mesh axis runs over, the one named last changes fastest.
Arguments:
- inputs: float32 [96, 256, 512], P(('dp', 'src')), may hold values from -6 to 6
- memory: float32 [96, 256, 512], P('dp', 'src'), may hold values from -6 to 6
- timesteps: int32 [96], P(('dp', 'src')), may hold values from 0 to 49
- mask_flags: int32 [96, 256], P(('dp', 'src')), may hold values from 0 to 1, as said below
- time_table: float32 [50, 512], replicated, may hold values from -3 to 3
- mask_vector: float32 [512], replicated, may hold values from -6 to 6
- first_gain: float32 [512], replicated, may hold values from 0.5 to 1.5
- first_bias: float32 [512], replicated, may hold values from -2 to 2
- self_qkv: float32 [512, 1536], replicated, may hold values from -0.25 to 0.25
- self_out: float32 [512, 512], replicated, may hold values from -1 to 1
- cross_query: float32 [512, 512], replicated, may hold values from -0.25 to 0.25
- cross_kv: float32 [512, 1024], replicated, may hold values from -0.25 to 0.25
- cross_out: float32 [512, 512], replicated, may hold values from -1 to 1
- second_gain: float32 [512], replicated, may hold values from 0.5 to 1.5
- second_bias: float32 [512], replicated, may hold values from -2 to 2
- expand_weight: float32 [512, 2048], replicated, may hold values from -0.25 to 0.25
- reduce_weight: float32 [2048, 512], replicated, may hold values from -0.125 to 0.125
- cotangent: float32 [96, 256, 512], P(('dp', 'src')), may hold values from -6 to 6
Outputs:
- output: float32 [96, 256, 512], P(('dp', 'src'))
- input_grad: float32 [96, 256, 512], P(('dp', 'src'))
- memory_grad: float32 [96, 256, 512], P('dp', 'src')
- time_grad: float32 [50, 512], replicated
- mask_grad: float32 [512], replicated
- first_gain_grad: float32 [512], replicated
- first_bias_grad: float32 [512], replicated
- self_qkv_grad: float32 [512, 1536], replicated
- self_out_grad: float32 [512, 512], replicated
- cross_query_grad: float32 [512, 512], replicated
- cross_kv_grad: float32 [512, 1024], replicated
- cross_out_grad: float32 [512, 512], replicated
- second_gain_grad: float32 [512], replicated
- second_bias_grad: float32 [512], replicated
- expand_grad: float32 [512, 2048], replicated
- reduce_grad: float32 [2048, 512], replicated
The draws below stay inside these ranges and needn't reach their ends.
Inputs may be any that keep to these rules, and one draw needn't show every extreme that they name: `mask_flags`: each item marks between 1 and 256 of its tokens.
All inputs are finite; a program needn't handle non-finite values.
Results may differ from the reference program's by a relative error of at most 0.0003.
Values sent between devices are 32-bit elements; how exact they have to be, the bound alone decides.
No kernel may reach another device: no remote copies, remote signals or barrier semaphores. Data moves between devices by JAX's collectives and lax.ppermute only.
A program may use at most 192 MiB of HBM per device.

```python
import math
import jax
import jax.numpy as jnp
from jax import lax

D = 512
HEADS = 8
FF = 2048
NSTEP = 50
LEN = 256
SLEN = 256
ITEMS = 96


def draw_mask_flags(key, part):
    key = jax.random.fold_in(key, 11)
    count_key, order_key = jax.random.split(key)
    counts = jax.random.randint(count_key, (ITEMS, 1), 1, LEN + 1)
    ranks = jax.random.permutation(order_key, jnp.broadcast_to(jnp.arange(LEN, dtype=jnp.int32), (ITEMS, LEN)), axis=1, independent=True)
    return (ranks < counts).astype(jnp.int32)


def with_ends(entries, rng, low, high):
    shape = entries.shape
    index_at = [jax.random.randint(jax.random.fold_in(rng, axis), (), 0, shape[axis]) for axis in range(len(shape))]
    entries = entries.at[tuple(index_at)].set(low)
    longest = shape.index(max(shape))
    index_at[longest] = (index_at[longest] + 1) % shape[longest]
    return entries.at[tuple(index_at)].set(high)


def levels(stream_key, extent, cuts, least, top_value):
    loudness = 1.0
    for position, shards_of in cuts:
        heights = jax.random.uniform(jax.random.fold_in(jax.random.fold_in(stream_key, 6), position), (shards_of,), jnp.float32, least / len(cuts), top_value / len(cuts))
        loudness = loudness * jnp.repeat(jnp.exp(heights), extent[position] // shards_of).reshape((-1,) + (1,) * (len(extent) - 1 - position))
    return loudness


def noise(key, dims, scale, limit, cuts=(), kind=jnp.bfloat16):
    gain = levels(key, dims, cuts, -0.22, 0.18) if cuts else 1.0
    values = jax.random.normal(key, dims, jnp.float32) * scale * gain
    return jnp.minimum(jnp.maximum(values, -limit), limit).astype(kind)


def setup_inputs(seed: int = 0) -> dict:
    keys = jax.random.split(jax.random.key(seed), 19)
    inputs = noise(keys[0], (ITEMS, LEN, D), 1.0, 6.0, ((0, 32),), jnp.float32)
    memory = noise(keys[1], (ITEMS, SLEN, D), 1.0, 6.0, ((0, 16), (1, 2)), jnp.float32)
    timesteps = with_ends(jax.random.randint(keys[2], (ITEMS,), 0, NSTEP), jax.random.fold_in(keys[2], 1), 0, NSTEP - 1).astype(jnp.int32)
    mask_flags = draw_mask_flags(jax.random.fold_in(keys[18], 71), 0)
    time_table = noise(keys[4], (NSTEP, D), 0.5, 3.0, (), jnp.float32)
    mask_vector = noise(keys[5], (D,), 1.0, 6.0, (), jnp.float32)
    first_gain = jnp.clip(1.0 + 0.1 * jax.random.normal(keys[6], (D,), jnp.float32), 0.5, 1.5)
    first_bias = noise(keys[7], (D,), 0.3, 2.0, (), jnp.float32)
    self_qkv = noise(keys[8], (D, 3 * D), D ** -0.5, 0.25, (), jnp.float32)
    self_out = noise(keys[9], (D, D), (D // 16) ** -0.5, 1.0, (), jnp.float32)
    cross_query = noise(keys[10], (D, D), D ** -0.5, 0.25, (), jnp.float32)
    cross_kv = noise(keys[11], (D, 2 * D), D ** -0.5, 0.25, (), jnp.float32)
    cross_out = noise(keys[12], (D, D), (D // 16) ** -0.5, 1.0, (), jnp.float32)
    second_gain = jnp.clip(1.0 + 0.1 * jax.random.normal(keys[13], (D,), jnp.float32), 0.5, 1.5)
    second_bias = noise(keys[14], (D,), 0.3, 2.0, (), jnp.float32)
    expand_weight = noise(keys[15], (D, FF), D ** -0.5, 0.25, (), jnp.float32)
    reduce_weight = noise(keys[16], (FF, D), FF ** -0.5, 0.125, (), jnp.float32)
    cotangent = noise(keys[17], (ITEMS, LEN, D), 1.0, 6.0, ((0, 32),), jnp.float32)
    return {"inputs": inputs, "memory": memory, "timesteps": timesteps, "mask_flags": mask_flags, "time_table": time_table, "mask_vector": mask_vector, "first_gain": first_gain, "first_bias": first_bias, "self_qkv": self_qkv, "self_out": self_out, "cross_query": cross_query, "cross_kv": cross_kv, "cross_out": cross_out, "second_gain": second_gain, "second_bias": second_bias, "expand_weight": expand_weight, "reduce_weight": reduce_weight, "cotangent": cotangent}


precise = lax.Precision.HIGHEST

@jax.custom_vjp
def low(v):
    return lax.optimization_barrier(v.astype(jnp.bfloat16)).astype(jnp.float32)

@jax.custom_vjp
def low_back(v):
    return v

def low_keep(v):
    return (low(v), None)

def low_pass(kept, grad):
    return (grad,)

def back_keep(v):
    return (v, None)

def back_low(kept, grad):
    return (low(grad),)
low.defvjp(low_keep, low_pass)
low_back.defvjp(back_keep, back_low)

def layer_norm(values, norm_gain, norm_bias):
    centred = values - lax.optimization_barrier(jnp.mean(values, -1, keepdims=True))
    inverse = lax.rsqrt(lax.optimization_barrier(jnp.mean(centred * centred, -1, keepdims=True)) + 1e-05)
    return centred * inverse * norm_gain + norm_bias

def heads_of(values):
    return values.reshape(values.shape[0], values.shape[1], HEADS, values.shape[2] // HEADS)

def attend(query_rows, key_rows, value_rows):
    query_heads = heads_of(query_rows)
    key_heads = heads_of(key_rows)
    value_heads = heads_of(value_rows)
    scores = jnp.einsum('bqhe,bkhe->bhqk', query_heads, key_heads, precision=precise) * query_heads.shape[-1] ** (-0.5)
    weights = jax.nn.softmax(scores, -1)
    result = jnp.einsum('bhqk,bkhe->bqhe', weights, value_heads, precision=precise)
    return result.reshape(query_rows.shape[0], query_rows.shape[1], query_rows.shape[2])

def layer(tokens, source, stamps, flags, params):
    time_table, mask_vector, first_gain, first_bias, self_qkv, self_out, cross_query, cross_kv, cross_out, second_gain, second_bias, expand_weight, reduce_weight = params
    width = tokens.shape[2]
    onehot = (stamps[:, None] == jnp.arange(time_table.shape[0], dtype=jnp.int32)[None, :]).astype(jnp.float32)
    chosen = flags.astype(jnp.float32)[..., None]
    start = tokens * (1.0 - chosen) + chosen * mask_vector + jnp.dot(onehot, time_table, precision=precise)[:, None, :]
    normed_one = layer_norm(start, first_gain, first_bias)
    packed = jnp.dot(normed_one, self_qkv, precision=precise)
    attended = attend(packed[..., :width], packed[..., width:2 * width], packed[..., 2 * width:])
    middle = start + jnp.dot(attended, self_out, precision=precise)
    cross_rows = jnp.dot(middle, cross_query, precision=precise)
    pairs = jnp.dot(source, cross_kv, precision=precise)
    crossed = attend(cross_rows, pairs[..., :width], pairs[..., width:])
    after_cross = middle + jnp.dot(crossed, cross_out, precision=precise)
    normed_two = layer_norm(after_cross, second_gain, second_bias)
    hidden = jax.nn.gelu(jnp.dot(normed_two, expand_weight, precision=precise), approximate=False)
    return after_cross + jnp.dot(hidden, reduce_weight, precision=precise)

def add_pair(earlier, later):
    return earlier + later

def reference(inputs, memory, timesteps, mask_flags, time_table, mask_vector, first_gain, first_bias, self_qkv, self_out, cross_query, cross_kv, cross_out, second_gain, second_bias, expand_weight, reduce_weight, cotangent):
    params = (time_table, mask_vector, first_gain, first_bias, self_qkv, self_out, cross_query, cross_kv, cross_out, second_gain, second_bias, expand_weight, reduce_weight)
    count = math.gcd(inputs.shape[0], 16)
    blocks = inputs.shape[0] // count

    def split(values):
        return values.reshape((blocks, count) + values.shape[1:])

    def one_block(totals, pieces):
        tokens, source, stamps, flags, upstream = pieces

        def forward(tokens_in, source_in, params_in):
            return layer(tokens_in, source_in, stamps, flags, params_in)
        result, pullback = jax.vjp(forward, tokens, source, params)
        token_grad, source_grad, param_grads = pullback(upstream)
        return (jax.tree.map(add_pair, totals, param_grads), (result, token_grad, source_grad))
    zeros = jax.tree.map(jnp.zeros_like, params)
    totals, (result, token_grad, source_grad) = lax.scan(one_block, zeros, (split(inputs), split(memory), split(timesteps), split(mask_flags), split(cotangent)))
    return (result.reshape(inputs.shape), token_grad.reshape(inputs.shape), source_grad.reshape(memory.shape), totals[0], totals[1], totals[2], totals[3], totals[4], totals[5], totals[6], totals[7], totals[8], totals[9], totals[10], totals[11], totals[12])
```

```python
import functools

import jax
import jax.numpy as jnp
from jax import lax
from jax.experimental import pallas as pl
from jax.experimental.pallas import tpu as pltpu
from jax.sharding import PartitionSpec as P

HEADS = 8
EPSILON = 1e-05
ALL = ("dp", "src")
f32 = jnp.float32
bf16 = jnp.bfloat16
VMEM_LIMIT = 56 * 2**20


def split(values):
    high = values.astype(bf16)
    return high, (values - high.astype(f32)).astype(bf16)


def dot(left, right, left_dim, right_dim):
    return lax.dot_general(
        left, right, (((left_dim,), (right_dim,)), ((), ())), preferred_element_type=f32
    )


def three(left, right, left_dim=1, right_dim=0):
    left_high, left_low = left
    right_high, right_low = right
    return (
        dot(left_high, right_high, left_dim, right_dim)
        + dot(left_high, right_low, left_dim, right_dim)
        + dot(left_low, right_high, left_dim, right_dim)
    )


def keep_split(ref, values):
    high, low = split(values)
    ref[0] = high
    ref[1] = low


def pair_of(ref):
    return ref[0], ref[1]


def norm(values):
    centred = values - jnp.mean(values, -1, keepdims=True)
    inverse = lax.rsqrt(jnp.mean(centred * centred, -1, keepdims=True) + EPSILON)
    return centred * inverse, inverse


def norm_back(grad_out, normed, inverse, gain):
    scaled = grad_out * gain
    return inverse * (
        scaled
        - jnp.mean(scaled, -1, keepdims=True)
        - normed * jnp.mean(scaled * normed, -1, keepdims=True)
    )


def half_masks(shape):
    lane = lax.broadcasted_iota(jnp.int32, shape, 1)
    size = shape[1] // 2
    return [lane < size, lane >= size]


def scores(masked, other):
    high, low = masked
    other_high, other_low = other
    return dot(
        jnp.concatenate([high, low], 1), jnp.concatenate([other_high, other_high], 1), 1, 1
    ) + dot(high, other_low, 1, 1)


def spread(weights, values, dim):
    high, low = weights
    value_high, value_low = values
    both = dot(high, jnp.concatenate([value_high, value_low], 1), dim, 0)
    size = value_high.shape[1]
    return both[:, :size] + both[:, size:] + dot(low, value_high, dim, 0)


def attend(queries, keys, values, weights_ref, out_ref):
    size = 2 * queries.shape[1] // HEADS
    masks = half_masks((queries.shape[0], size))
    key_masks = half_masks((keys.shape[0], size))
    scale = (size // 2) ** (-0.5)
    for pair in range(HEADS // 2):
        lanes = slice(pair * size, (pair + 1) * size)
        pair_queries = queries[:, lanes] * scale
        pair_keys = split(keys[:, lanes])
        pair_values = values[:, lanes]
        total = 0.0
        for e in range(2):
            score = scores(split(jnp.where(masks[e], pair_queries, 0.0)), pair_keys)
            exponent = jnp.exp(score - jnp.max(score, -1, keepdims=True))
            weights = exponent * (1.0 / jnp.sum(exponent, -1, keepdims=True))
            weights_ref[0, 2 * pair + e] = weights
            total = total + spread(
                split(weights), split(jnp.where(key_masks[e], pair_values, 0.0)), 1
            )
        out_ref[:, lanes] = total


def attend_back(queries, keys, values, weights_ref, grad, attended, put):
    size = 2 * queries.shape[1] // HEADS
    masks = half_masks((queries.shape[0], size))
    key_masks = half_masks((keys.shape[0], size))
    scale = (size // 2) ** (-0.5)
    for pair in range(HEADS // 2):
        lanes = slice(pair * size, (pair + 1) * size)
        pair_queries = queries[:, lanes] * scale
        pair_keys = keys[:, lanes]
        pair_values = split(values[:, lanes])
        pair_grad = grad[:, lanes]
        pair_dots = pair_grad * attended[:, lanes]
        grad_queries = grad_keys = grad_values = 0.0
        for e in range(2):
            head_grad = split(jnp.where(masks[e], pair_grad, 0.0))
            dots = jnp.sum(jnp.where(masks[e], pair_dots, 0.0), -1, keepdims=True)
            weights = weights_ref[0, 2 * pair + e]
            grad_scores = split(weights * (scores(head_grad, pair_values) - dots))
            grad_queries = grad_queries + spread(
                grad_scores, split(jnp.where(key_masks[e], pair_keys, 0.0)), 1
            )
            grad_keys = grad_keys + spread(
                grad_scores, split(jnp.where(masks[e], pair_queries, 0.0)), 0
            )
            grad_values = grad_values + spread(split(weights), head_grad, 0)
        put(lanes, grad_queries * scale, grad_keys, grad_values)


def self_forward(
    stamps,
    inputs,
    chosen,
    time_table,
    mask_vector,
    gain,
    bias,
    qkv_weight,
    out_weight,
    query_weight,
    normed_out,
    inverse_out,
    qkv_out,
    weights_out,
    attended_out,
    middle_out,
    query_out,
    qkv_split,
    out_split,
    query_split,
):
    item = pl.program_id(0)

    @pl.when(item == 0)
    def _():
        keep_split(qkv_split, qkv_weight[...])
        keep_split(out_split, out_weight[...])
        keep_split(query_split, query_weight[...])

    flags = chosen[0]
    start = (
        inputs[0] * (1.0 - flags)
        + flags * mask_vector[...]
        + time_table[pl.ds(stamps[item], 1), :]
    )
    normed, inverse = norm(start)
    normed_out[0] = normed
    inverse_out[0] = inverse
    packed = three(split(normed * gain[...] + bias[...]), pair_of(qkv_split))
    qkv_out[0] = packed
    width = start.shape[1]
    attend(
        packed[:, :width],
        packed[:, width : 2 * width],
        packed[:, 2 * width :],
        weights_out,
        attended_out.at[0],
    )
    middle = start + three(split(attended_out[0]), pair_of(out_split))
    middle_out[0] = middle
    query_out[0] = three(split(middle), pair_of(query_split))


def cross_forward(
    place,
    memory_own,
    memory_far,
    queries,
    middle,
    kv_weight,
    out_weight,
    kv_out,
    weights_out,
    attended_out,
    after_out,
    kv_split,
    out_split,
):
    @pl.when(pl.program_id(0) == 0)
    def _():
        keep_split(kv_split, kv_weight[...])
        keep_split(out_split, out_weight[...])

    memory = jnp.concatenate([memory_own[0], memory_far[0]], 0)
    pairs = three(split(memory), pair_of(kv_split))
    kv_out[0] = pairs
    width = memory.shape[1]
    attend(queries[0], pairs[:, :width], pairs[:, width:], weights_out, attended_out.at[0])
    after_out[0] = middle[0] + three(split(attended_out[0]), pair_of(out_split))


def feed(
    first,
    last,
    after,
    cotangent,
    gain,
    bias,
    expand,
    reduce,
    total_in,
    grad_in,
    total_out,
    grad_out,
    weight_grads,
    gain_grad,
    bias_grad,
    normed_split,
    cot_split,
    total,
    grad_normed,
):
    step = pl.program_id(0)

    @pl.when(step == 0)
    def _():
        normed, _ = norm(after[...])
        keep_split(normed_split, normed * gain[...] + bias[...])
        keep_split(cot_split, cotangent[...])
        if first:
            total[...] = after[...]
            grad_normed[...] = jnp.zeros_like(grad_normed)
        else:
            total[...] = total_in[...]
            grad_normed[...] = grad_in[...]

    width = after.shape[1]
    size = 256
    for k in range(expand.shape[1] // size):
        cols = slice(k * size, (k + 1) * size)
        expand_pair = split(expand[:, cols])
        reduce_pair = split(reduce[cols, :])
        pre = three(pair_of(normed_split), expand_pair)
        cdf = 0.5 * (1.0 + lax.erf(pre * (0.5**0.5)))
        slope = cdf + pre * (jnp.exp(-0.5 * pre * pre) * 0.3989422804014327)
        hidden = split(pre * cdf)
        total[...] += three(hidden, reduce_pair)
        weight_grads[0, 0, cols, :] = three(hidden, pair_of(cot_split), 0, 0)
        grad_pre = split(three(pair_of(cot_split), reduce_pair, 1, 1) * slope)
        weight_grads[0, 1, :, cols] = three(pair_of(normed_split), grad_pre, 0, 0)
        grad_normed[...] += three(grad_pre, expand_pair, 1, 1)

    @pl.when(step == pl.num_programs(0) - 1)
    def _():
        total_out[...] = total[...]
        if last:
            normed, inverse = norm(after[...])
            grad = grad_normed[...]
            gain_grad[...] = jnp.sum(grad * normed, 0, keepdims=True)
            bias_grad[...] = jnp.sum(grad, 0, keepdims=True)
            grad_out[...] = cotangent[...] + norm_back(grad, normed, inverse, gain[...])
        else:
            grad_out[...] = grad_normed[...]


def cross_backward(
    place,
    memory_own,
    memory_far,
    queries,
    middle,
    pairs,
    weights,
    attended,
    grad_after,
    out_weight,
    query_weight,
    kv_weight,
    own_grad,
    far_grad,
    middle_grad,
    weight_grads,
    out_split,
    query_split,
    kv_split,
    grad_queries,
    grad_pairs,
):
    item = pl.program_id(0)

    @pl.when(item == 0)
    def _():
        keep_split(out_split, out_weight[...])
        keep_split(query_split, query_weight[...])
        keep_split(kv_split, kv_weight[...])
        weight_grads[...] = jnp.zeros_like(weight_grads)

    width = middle.shape[2]
    upstream = grad_after[0]
    upstream_pair = split(upstream)
    grad = three(upstream_pair, pair_of(out_split), 1, 1)
    weight_grads[0] += three(split(attended[0]), upstream_pair, 0, 0)

    def put(lanes, query_part, key_part, value_part):
        grad_queries[:, lanes] = query_part
        grad_pairs[:, lanes] = key_part
        grad_pairs[:, lanes.start + width : lanes.stop + width] = value_part

    attend_back(
        queries[0],
        pairs[0, :, :width],
        pairs[0, :, width:],
        weights,
        grad,
        attended[0],
        put,
    )
    query_pair = split(grad_queries[...])
    middle_grad[0] = upstream + three(query_pair, pair_of(query_split), 1, 1)
    weight_grads[1] += three(split(middle[0]), query_pair, 0, 0)
    both = split(grad_pairs[...])
    memory_grad = three(both, pair_of(kv_split), 1, 1)
    half = own_grad.shape[1]
    own_grad[0] = memory_grad[:half]
    far_grad[0] = memory_grad[half:]
    memory_pair = split(jnp.concatenate([memory_own[0], memory_far[0]], 0))
    for k in range(2):
        cols = slice(k * width, (k + 1) * width)
        weight_grads[2 + k] += three(memory_pair, (both[0][:, cols], both[1][:, cols]), 0, 0)


def self_backward(
    stamps,
    normed,
    inverse,
    chosen,
    packed,
    weights,
    attended,
    grad_middle,
    gain,
    bias,
    qkv_weight,
    out_weight,
    input_grad,
    weight_grads,
    time_grad,
    mask_grad,
    gain_grad,
    bias_grad,
    qkv_split,
    out_split,
    grad_packed,
):
    item = pl.program_id(0)

    @pl.when(item == 0)
    def _():
        keep_split(out_split, out_weight[...])
        keep_split(qkv_split, qkv_weight[...])
        for ref in (weight_grads, time_grad, mask_grad, gain_grad, bias_grad):
            ref[...] = jnp.zeros_like(ref)

    width = normed.shape[2]
    upstream = grad_middle[0]
    upstream_pair = split(upstream)
    grad = three(upstream_pair, pair_of(out_split), 1, 1)
    weight_grads[0] += three(split(attended[0]), upstream_pair, 0, 0)

    def put(lanes, query_part, key_part, value_part):
        for k, part in enumerate((query_part, key_part, value_part)):
            grad_packed[:, lanes.start + k * width : lanes.stop + k * width] = part

    attend_back(
        packed[0, :, :width],
        packed[0, :, width : 2 * width],
        packed[0, :, 2 * width :],
        weights,
        grad,
        attended[0],
        put,
    )
    all_three = split(grad_packed[...])
    grad_normed = three(all_three, pair_of(qkv_split), 1, 1)
    unit = normed[0]
    normed_pair = split(unit * gain[...] + bias[...])
    for k in range(3):
        cols = slice(k * width, (k + 1) * width)
        weight_grads[1 + k] += three(
            normed_pair, (all_three[0][:, cols], all_three[1][:, cols]), 0, 0
        )
    gain_grad[...] += jnp.sum(grad_normed * unit, 0, keepdims=True)
    bias_grad[...] += jnp.sum(grad_normed, 0, keepdims=True)
    grad_start = upstream + norm_back(grad_normed, unit, inverse[0], gain[...])
    flags = chosen[0]
    input_grad[0] = grad_start * (1.0 - flags)
    mask_grad[...] += jnp.sum(grad_start * flags, 0, keepdims=True)
    row = pl.ds(stamps[item], 1)
    time_grad[row, :] += jnp.sum(grad_start, 0, keepdims=True)


def whole_spec(shape):
    return pl.BlockSpec(shape, lambda i, *_: (0,) * len(shape))


def item_spec(shape):
    return pl.BlockSpec((1,) + shape[1:], lambda i, *_: (i,) + (0,) * (len(shape) - 1))


def own_spec(shape, items):
    return pl.BlockSpec((1,) + shape[1:], lambda i, place: (place[0] * items + i, 0, 0))


def struct(*shape):
    return jax.ShapeDtypeStruct(shape, f32)


def call(kernel, grid, prefetch, ins, outs, scratch, flops, name):
    return pl.pallas_call(
        kernel,
        grid_spec=pltpu.PrefetchScalarGridSpec(
            num_scalar_prefetch=len(prefetch),
            grid=(grid,),
            in_specs=[spec for _, spec in ins],
            out_specs=[spec for _, spec in outs],
            scratch_shapes=scratch,
        ),
        out_shape=[out for out, _ in outs],
        compiler_params=pltpu.CompilerParams(
            dimension_semantics=("arbitrary",), vmem_limit_bytes=VMEM_LIMIT
        ),
        cost_estimate=pl.CostEstimate(flops=flops, bytes_accessed=0, transcendentals=0),
        name=name,
    )(*prefetch, *[array for array, _ in ins])


def split_scratch(*shape):
    return pltpu.VMEM((2,) + shape, bf16)


def whole(array):
    return (array, whole_spec(array.shape))


def by_item(array):
    return (array, item_spec(array.shape))


def shards(
    inputs,
    memory,
    timesteps,
    mask_flags,
    time_table,
    mask_vector,
    first_gain,
    first_bias,
    self_qkv,
    self_out,
    cross_query,
    cross_kv,
    cross_out,
    second_gain,
    second_bias,
    expand_weight,
    reduce_weight,
    cotangent,
):
    items, length, width = inputs.shape
    half = memory.shape[1]
    positions = 2 * half
    feed_width = expand_weight.shape[1]
    mac = items * length * width * width
    swap = [(0, 1), (1, 0)]
    src = lax.axis_index("src")
    place = src.astype(jnp.int32).reshape(1)

    memory_far = lax.ppermute(
        lax.dynamic_slice_in_dim(memory, (1 - src) * items, items, 0), "src", swap
    )
    chosen = mask_flags.astype(f32)[..., None]
    vectors = [v[None, :] for v in (mask_vector, first_gain, first_bias, second_gain, second_bias)]
    mask_row, first_gain_row, first_bias_row, second_gain_row, second_bias_row = vectors

    def rows_out(*shape):
        return (struct(*shape), item_spec(shape))

    def whole_out(*shape):
        return (struct(*shape), whole_spec(shape))

    normed, inverse, packed, self_weights, self_attended, middle, queries = call(
        self_forward,
        items,
        [timesteps],
        [
            by_item(inputs),
            by_item(chosen),
            whole(time_table),
            whole(mask_row),
            whole(first_gain_row),
            whole(first_bias_row),
            whole(self_qkv),
            whole(self_out),
            whole(cross_query),
        ],
        [
            rows_out(items, length, width),
            rows_out(items, length, 1),
            rows_out(items, length, 3 * width),
            rows_out(items, HEADS, length, length),
            rows_out(items, length, width),
            rows_out(items, length, width),
            rows_out(items, length, width),
        ],
        [
            split_scratch(width, 3 * width),
            split_scratch(width, width),
            split_scratch(width, width),
        ],
        6 * 6 * mac,
        "self_forward",
    )
    pairs, cross_weights, cross_attended, after = call(
        cross_forward,
        items,
        [place],
        [
            (memory, own_spec(memory.shape, items)),
            by_item(memory_far),
            by_item(queries),
            by_item(middle),
            whole(cross_kv),
            whole(cross_out),
        ],
        [
            rows_out(items, positions, 2 * width),
            rows_out(items, HEADS, length, positions),
            rows_out(items, length, width),
            rows_out(items, length, width),
        ],
        [split_scratch(width, 2 * width), split_scratch(width, width)],
        6 * 4 * mac,
        "cross_forward",
    )

    tokens = items * length
    after_flat = after.reshape(tokens, width)
    cot_flat = cotangent.reshape(tokens, width)
    blocks = feed_width // width
    part = blocks // 2
    total = grad = jnp.zeros((8, 128), f32)
    feed_grads = []
    for k in range(2):
        total, grad, weight_grads, second_gain_g, second_bias_g = call(
            functools.partial(feed, k == 0, k == 1),
            part,
            [],
            [
                whole(after_flat),
                whole(cot_flat),
                whole(second_gain_row),
                whole(second_bias_row),
                (
                    expand_weight,
                    pl.BlockSpec((width, width), lambda j, k=k: (0, j + k * part)),
                ),
                (
                    reduce_weight,
                    pl.BlockSpec((width, width), lambda j, k=k: (j + k * part, 0)),
                ),
                whole(total),
                whole(grad),
            ],
            [
                whole_out(tokens, width),
                whole_out(tokens, width),
                (
                    struct(part, 2, width, width),
                    pl.BlockSpec((1, 2, width, width), lambda j: (j, 0, 0, 0)),
                ),
                whole_out(1, width),
                whole_out(1, width),
            ],
            [
                split_scratch(tokens, width),
                split_scratch(tokens, width),
                pltpu.VMEM((tokens, width), f32),
                pltpu.VMEM((tokens, width), f32),
            ],
            6 * 12 * mac,
            f"feed_{k}",
        )
        feed_grads.append(weight_grads)
    output = total.reshape(items, length, width)
    grad_after = grad.reshape(items, length, width)

    memory_grad, far_grad, grad_middle, cross_grads = call(
        cross_backward,
        items,
        [place],
        [
            (memory, own_spec(memory.shape, items)),
            by_item(memory_far),
            by_item(queries),
            by_item(middle),
            by_item(pairs),
            by_item(cross_weights),
            by_item(cross_attended),
            by_item(grad_after),
            whole(cross_out),
            whole(cross_query),
            whole(cross_kv),
        ],
        [
            (struct(*memory.shape), own_spec(memory.shape, items)),
            rows_out(items, half, width),
            rows_out(items, length, width),
            whole_out(4, width, width),
        ],
        [
            split_scratch(width, width),
            split_scratch(width, width),
            split_scratch(width, 2 * width),
            pltpu.VMEM((length, width), f32),
            pltpu.VMEM((positions, 2 * width), f32),
        ],
        6 * 10 * mac,
        "cross_backward",
    )
    far_grad = lax.ppermute(far_grad, "src", swap)
    memory_grad = lax.dynamic_update_slice_in_dim(memory_grad, far_grad, (1 - src) * items, 0)

    steps = time_table.shape[0]
    input_grad, self_grads, time_g, mask_g, first_gain_g, first_bias_g = call(
        self_backward,
        items,
        [timesteps],
        [
            by_item(normed),
            by_item(inverse),
            by_item(chosen),
            by_item(packed),
            by_item(self_weights),
            by_item(self_attended),
            by_item(grad_middle),
            whole(first_gain_row),
            whole(first_bias_row),
            whole(self_qkv),
            whole(self_out),
        ],
        [
            rows_out(items, length, width),
            whole_out(4, width, width),
            whole_out(steps, width),
            whole_out(1, width),
            whole_out(1, width),
            whole_out(1, width),
        ],
        [
            split_scratch(width, 3 * width),
            split_scratch(width, width),
            pltpu.VMEM((length, 3 * width), f32),
        ],
        6 * 10 * mac,
        "self_backward",
    )

    small = jnp.concatenate([mask_g, first_gain_g, first_bias_g, second_gain_g, second_bias_g, time_g])
    groups = [
        feed_grads[0].reshape(-1, width),
        feed_grads[1].reshape(-1, width),
        cross_grads.reshape(-1, width),
        self_grads.reshape(-1, width),
    ]
    first, second, third, fourth, small = lax.psum((*groups, small), ALL)
    fed = jnp.concatenate([first.reshape(part, 2, width, width), second.reshape(part, 2, width, width)])
    reduce_g = fed[:, 0].reshape(feed_width, width)
    expand_g = jnp.transpose(fed[:, 1], (1, 0, 2)).reshape(width, feed_width)
    third = third.reshape(4, width, width)
    fourth = fourth.reshape(4, width, width)
    cross_kv_g = jnp.concatenate([third[2], third[3]], 1)
    self_qkv_g = jnp.concatenate([fourth[1], fourth[2], fourth[3]], 1)
    return (
        output,
        input_grad,
        memory_grad,
        small[5:],
        small[0],
        small[1],
        small[2],
        self_qkv_g,
        fourth[0],
        third[1],
        cross_kv_g,
        third[0],
        small[3],
        small[4],
        expand_g,
        reduce_g,
    )


def solution(mesh):
    tokens = P(("dp", "src"), None, None)
    placed = (tokens, P("dp", "src", None), P(("dp", "src")), P(("dp", "src"), None))
    return jax.shard_map(
        shards,
        mesh=mesh,
        in_specs=placed + (P(),) * 13 + (tokens,),
        out_specs=(tokens, tokens, P("dp", "src", None)) + (P(),) * 13,
        check_vma=False,
    )
```

```python
import functools

import jax
import jax.numpy as jnp
from jax import lax
from jax.experimental import pallas as pl
from jax.experimental.pallas import tpu as pltpu
from jax.sharding import PartitionSpec as P

HEADS = 8
EPSILON = 1e-05
ALL = ("dp", "src")
f32 = jnp.float32
bf16 = jnp.bfloat16
VMEM_LIMIT = 56 * 2**20


def split(values):
    high = values.astype(bf16)
    return high, (values - high.astype(f32)).astype(bf16)


def dot(left, right, left_dim, right_dim):
    return lax.dot_general(
        left, right, (((left_dim,), (right_dim,)), ((), ())), preferred_element_type=f32
    )


def three(left, right, left_dim=1, right_dim=0):
    left_high, left_low = left
    right_high, right_low = right
    return (
        dot(left_high, right_high, left_dim, right_dim)
        + dot(left_high, right_low, left_dim, right_dim)
        + dot(left_low, right_high, left_dim, right_dim)
    )


def keep_split(ref, values):
    high, low = split(values)
    ref[0] = high
    ref[1] = low


def pair_of(ref):
    return ref[0], ref[1]


def upright(row):
    n = row.shape[1]
    same = lax.broadcasted_iota(jnp.int32, (n, n), 0) == lax.broadcasted_iota(jnp.int32, (n, n), 1)
    spread_row = jnp.broadcast_to(row.astype(f32), (n, n))
    return jnp.sum(jnp.where(same, spread_row, 0.0), -1, keepdims=True)


def norm(values):
    centred = values - jnp.mean(values, -1, keepdims=True)
    inverse = lax.rsqrt(jnp.mean(centred * centred, -1, keepdims=True) + EPSILON)
    return centred * inverse, inverse


def norm_back(grad_out, normed, inverse, gain):
    scaled = grad_out * gain
    return inverse * (
        scaled
        - jnp.mean(scaled, -1, keepdims=True)
        - normed * jnp.mean(scaled * normed, -1, keepdims=True)
    )


def stacked(values):
    lane = lax.broadcasted_iota(jnp.int32, values.shape, 1)
    first = lane < values.shape[1] // 2
    return split(
        jnp.concatenate([jnp.where(first, values, 0.0), jnp.where(first, 0.0, values)], 0)
    )


def scores(left, both):
    high, low = left
    both_high, both_low = both
    return dot(
        jnp.concatenate([high, low], 1), jnp.concatenate([both_high, both_high], 1), 1, 1
    ) + dot(high, both_low, 1, 1)


def spread(weights, values, dim):
    high, low = weights
    value_high, value_low = values
    both = dot(high, jnp.concatenate([value_high, value_low], 1), dim, 0)
    size = value_high.shape[1]
    return both[:, :size] + both[:, size:] + dot(low, value_high, dim, 0)


def own_lanes(values):
    n = values.shape[0] // 2
    lane = lax.broadcasted_iota(jnp.int32, (n, values.shape[1]), 1)
    return jnp.where(lane < values.shape[1] // 2, values[:n], values[n:])


def attend(queries, keys, values, weights_ref, out_ref):
    size = 2 * queries.shape[1] // HEADS
    count = keys.shape[0]
    scale = (size // 2) ** (-0.5)
    first = lax.broadcasted_iota(jnp.int32, (queries.shape[0], size), 1) < size // 2
    first_keys = lax.broadcasted_iota(jnp.int32, (count, size), 1) < size // 2
    for pair in range(HEADS // 2):
        lanes = slice(pair * size, (pair + 1) * size)
        pair_queries = queries[:, lanes] * scale
        pair_keys = split(keys[:, lanes])
        pair_values = values[:, lanes]
        total = 0.0
        for e in range(2):
            own = first if e == 0 else jnp.logical_not(first)
            own_keys = first_keys if e == 0 else jnp.logical_not(first_keys)
            score = scores(split(jnp.where(own, pair_queries, 0.0)), pair_keys)
            exponent = jnp.exp(score - jnp.max(score, -1, keepdims=True))
            weights = exponent * (1.0 / jnp.sum(exponent, -1, keepdims=True))
            weights_ref[0, pair, :, e * count : (e + 1) * count] = weights
            total = total + spread(
                split(weights), split(jnp.where(own_keys, pair_values, 0.0)), 1
            )
        out_ref[:, lanes] = total


def attend_back(queries, keys, values, weights_ref, grad, attended, put):
    size = 2 * queries.shape[1] // HEADS
    count = keys.shape[0]
    scale = (size // 2) ** (-0.5)
    first = lax.broadcasted_iota(jnp.int32, (queries.shape[0], size), 1) < size // 2
    for pair in range(HEADS // 2):
        lanes = slice(pair * size, (pair + 1) * size)
        pair_grad = grad[:, lanes]
        grad_pair = split(pair_grad)
        products = pair_grad * attended[:, lanes]
        weights = weights_ref[0, pair]
        grad_weights = scores(grad_pair, stacked(values[:, lanes]))
        parts = []
        for e in range(2):
            own = first if e == 0 else jnp.logical_not(first)
            dots = jnp.sum(jnp.where(own, products, 0.0), -1, keepdims=True)
            cols = slice(e * count, (e + 1) * count)
            parts.append(weights[:, cols] * (grad_weights[:, cols] - dots))
        grad_scores = split(jnp.concatenate(parts, 1))
        grad_queries = spread(grad_scores, stacked(keys[:, lanes]), 1)
        grad_keys = own_lanes(spread(grad_scores, split(queries[:, lanes] * scale), 0))
        grad_values = own_lanes(spread(split(weights), grad_pair, 0))
        put(lanes, grad_queries * scale, grad_keys, grad_values)


def self_forward(
    stamps,
    inputs,
    chosen,
    time_table,
    mask_vector,
    gain,
    bias,
    qkv_weight,
    out_weight,
    query_weight,
    normed_out,
    inverse_out,
    qkv_out,
    weights_out,
    attended_out,
    middle_out,
    query_out,
    qkv_split,
    out_split,
    query_split,
):
    item = pl.program_id(0)

    @pl.when(item == 0)
    def _():
        keep_split(qkv_split, qkv_weight[...])
        keep_split(out_split, out_weight[...])
        keep_split(query_split, query_weight[...])

    flags = upright(chosen[0])
    start = (
        inputs[0] * (1.0 - flags)
        + flags * mask_vector[...]
        + time_table[pl.ds(stamps[item], 1), :]
    )
    normed, inverse = norm(start)
    normed_out[0] = normed
    inverse_out[0] = inverse
    packed = three(split(normed * gain[...] + bias[...]), pair_of(qkv_split))
    qkv_out[0] = packed
    width = start.shape[1]
    attend(
        packed[:, :width],
        packed[:, width : 2 * width],
        packed[:, 2 * width :],
        weights_out,
        attended_out.at[0],
    )
    middle = start + three(split(attended_out[0]), pair_of(out_split))
    middle_out[0] = middle
    query_out[0] = three(split(middle), pair_of(query_split))


def cross_forward(
    place,
    memory_own,
    memory_far,
    queries,
    middle,
    kv_weight,
    out_weight,
    memory_out,
    kv_out,
    weights_out,
    attended_out,
    after_out,
    kv_split,
    out_split,
):
    @pl.when(pl.program_id(0) == 0)
    def _():
        keep_split(kv_split, kv_weight[...])
        keep_split(out_split, out_weight[...])

    memory = jnp.concatenate([memory_own[0], memory_far[0]], 0)
    memory_out[0] = memory
    pairs = three(split(memory), pair_of(kv_split))
    kv_out[0] = pairs
    width = memory.shape[1]
    attend(queries[0], pairs[:, :width], pairs[:, width:], weights_out, attended_out.at[0])
    after_out[0] = middle[0] + three(split(attended_out[0]), pair_of(out_split))


def feed(
    after,
    cotangent,
    attended,
    gain,
    bias,
    expand,
    reduce,
    output,
    grad_after,
    reduce_grad,
    expand_grad,
    out_grad,
    gain_grad,
    bias_grad,
    normed_split,
    cot_split,
):
    step = pl.program_id(0)
    last = pl.num_programs(0) - 1

    @pl.when(step == 0)
    def _():
        normed, _ = norm(after[...])
        keep_split(normed_split, normed * gain[...] + bias[...])
        keep_split(cot_split, cotangent[...])
        output[...] = after[...]
        grad_after[...] = jnp.zeros_like(grad_after)

    @pl.when(step < last)
    def _():
        expand_pair = split(expand[...])
        reduce_pair = split(reduce[...])
        pre = three(pair_of(normed_split), expand_pair)
        grad_hidden = three(pair_of(cot_split), reduce_pair, 1, 1)
        cdf = 0.5 * (1.0 + lax.erf(pre * (0.5**0.5)))
        slope = cdf + pre * (jnp.exp(-0.5 * pre * pre) * 0.3989422804014327)
        hidden = split(pre * cdf)
        output[...] += three(hidden, reduce_pair)
        reduce_grad[...] = three(hidden, pair_of(cot_split), 0, 0)
        grad_pre = split(grad_hidden * slope)
        expand_grad[...] = three(pair_of(normed_split), grad_pre, 0, 0)
        grad_after[...] += three(grad_pre, expand_pair, 1, 1)

    @pl.when(step == last)
    def _():
        normed, inverse = norm(after[...])
        grad = grad_after[...]
        gain_grad[...] = jnp.sum(grad * normed, 0, keepdims=True)
        bias_grad[...] = jnp.sum(grad, 0, keepdims=True)
        grad = cotangent[...] + norm_back(grad, normed, inverse, gain[...])
        grad_after[...] = grad
        out_grad[...] = three(split(attended[...]), split(grad), 0, 0)


def cross_backward(
    queries,
    pairs,
    weights,
    attended,
    grad_after,
    out_weight,
    query_weight,
    kv_weight,
    own_grad,
    far_grad,
    middle_grad,
    grad_queries,
    grad_pairs,
    out_split,
    query_split,
    kv_split,
):
    @pl.when(pl.program_id(0) == 0)
    def _():
        keep_split(out_split, out_weight[...])
        keep_split(query_split, query_weight[...])
        keep_split(kv_split, kv_weight[...])

    width = queries.shape[2]
    upstream = grad_after[0]
    grad = three(split(upstream), pair_of(out_split), 1, 1)

    def put(lanes, query_part, key_part, value_part):
        grad_queries[0, :, lanes] = query_part
        grad_pairs[0, :, lanes] = key_part
        grad_pairs[0, :, lanes.start + width : lanes.stop + width] = value_part

    attend_back(
        queries[0],
        pairs[0, :, :width],
        pairs[0, :, width:],
        weights,
        grad,
        attended[0],
        put,
    )
    middle_grad[0] = upstream + three(split(grad_queries[0]), pair_of(query_split), 1, 1)
    memory_grad = three(split(grad_pairs[0]), pair_of(kv_split), 1, 1)
    half = own_grad.shape[1]
    own_grad[0] = memory_grad[:half]
    far_grad[0] = memory_grad[half:]


def cross_weights(middle, grad_queries, memory, grad_pairs, self_attended, grad_middle, out):
    step = pl.program_id(0)

    def product(left, right):
        out[...] = three(split(left[...]), split(right[...]), 0, 0)

    pl.when(step == 0)(lambda: product(middle, grad_queries))
    pl.when((step == 1) | (step == 2))(lambda: product(memory, grad_pairs))
    pl.when(step == 3)(lambda: product(self_attended, grad_middle))


def self_backward(
    packed,
    weights,
    attended,
    grad_middle,
    out_weight,
    grad_packed,
    out_split,
):
    @pl.when(pl.program_id(0) == 0)
    def _():
        keep_split(out_split, out_weight[...])

    width = attended.shape[2]
    grad = three(split(grad_middle[0]), pair_of(out_split), 1, 1)

    def put(lanes, query_part, key_part, value_part):
        for k, part in enumerate((query_part, key_part, value_part)):
            grad_packed[0, :, lanes.start + k * width : lanes.stop + k * width] = part

    attend_back(
        packed[0, :, :width],
        packed[0, :, width : 2 * width],
        packed[0, :, 2 * width :],
        weights,
        grad,
        attended[0],
        put,
    )


def self_weights(normed, gain, bias, grad_packed, out, normed_split):
    @pl.when(pl.program_id(0) == 0)
    def _():
        keep_split(normed_split, normed[...] * gain[...] + bias[...])

    out[...] = three(pair_of(normed_split), split(grad_packed[...]), 0, 0)


def start_backward(
    stamps,
    normed,
    inverse,
    chosen,
    grad_packed,
    grad_middle,
    gain,
    qkv_weight,
    input_grad,
    time_grad,
    mask_grad,
    gain_grad,
    bias_grad,
    qkv_split,
):
    item = pl.program_id(0)

    @pl.when(item == 0)
    def _():
        keep_split(qkv_split, qkv_weight[...])
        for ref in (time_grad, mask_grad, gain_grad, bias_grad):
            ref[...] = jnp.zeros_like(ref)

    grad_normed = three(split(grad_packed[0]), pair_of(qkv_split), 1, 1)
    unit = normed[0]
    gain_grad[...] += jnp.sum(grad_normed * unit, 0, keepdims=True)
    bias_grad[...] += jnp.sum(grad_normed, 0, keepdims=True)
    grad_start = grad_middle[0] + norm_back(grad_normed, unit, inverse[0], gain[...])
    flags = upright(chosen[0])
    input_grad[0] = grad_start * (1.0 - flags)
    mask_grad[...] += jnp.sum(grad_start * flags, 0, keepdims=True)
    row = pl.ds(stamps[item], 1)
    time_grad[row, :] += jnp.sum(grad_start, 0, keepdims=True)


def exchange(values, kind, offset=1):
    groups, halves = lax.axis_size("dp"), lax.axis_size("src")
    shift = {"core": offset, "x": 2 * offset, "z": 4 * offset, "y": 0}[kind]
    pairs = []
    for d in range(groups):
        for s in range(halves):
            target = d * halves + (s ^ 1) if kind == "y" else (d ^ shift) * halves + s
            pairs.append((d * halves + s, target))
    return lax.ppermute(values, ALL, pairs)


def take(values, dim, index):
    return lax.dynamic_index_in_dim(values, index, dim, keepdims=False)


def place_of():
    group = lax.axis_index("dp")
    return group & 1, (group >> 1) & 1, lax.axis_index("src"), (group >> 2) & 3


def doubled(values, received, bit):
    return jnp.where(
        bit == 0, jnp.concatenate([values, received]), jnp.concatenate([received, values])
    )


class Sum:
    def __init__(self, values):
        self.steps = self.run(values)
        self.sends = next(self.steps)

    def run(self, values):
        core, x, y, z = place_of()
        rows, width = values.shape
        values = values.reshape(2, rows // 2, width)
        (received,) = yield [(take(values, 0, 1 - core), "core", 1)]
        values = take(values, 0, core) + received
        values = values.reshape(2, 2, 2, 4, rows // 64, width)
        one, two = values[0], values[1]
        for first, second, bit, other in (("x", "y", x, y), ("y", "x", y, x)):
            got_one, got_two = yield [
                (take(one, 0, 1 - bit), first, 1),
                (take(two, 0, 1 - other), second, 1),
            ]
            one = take(one, 0, bit) + got_one
            two = take(two, 0, other) + got_two
        both = jnp.stack([one, two])
        got = yield [(take(both, 1, z ^ k), "z", k) for k in (1, 2, 3)]
        share = take(both, 1, z) + got[0] + got[1] + got[2]
        offset = 4
        while 4 * offset < lax.axis_size("dp"):
            share = share + exchange(share, "z", offset)
            offset *= 2
        got = yield [(share, "z", k) for k in (1, 2, 3)]
        parts = [share, *got]

        def at(k):
            found = parts[0]
            for j in (1, 2, 3):
                found = jnp.where((z ^ j) == k, parts[j], found)
            return found

        both = jnp.stack([at(k) for k in range(4)], 1)
        one, two = both[0].reshape(rows // 16, width), both[1].reshape(rows // 16, width)
        got_one, got_two = yield [(one, "y", 1), (two, "x", 1)]
        self.halves = (doubled(one, got_one, y), doubled(two, got_two, x))
        yield []

    def put(self, received):
        self.sends = self.steps.send(received)


class End(Sum):
    def __init__(self, halves):
        self.steps = self.finish(*halves)
        self.sends = next(self.steps)

    def finish(self, one, two):
        _, x, y, _ = place_of()
        got_one, got_two = yield [(one, "x", 1), (two, "y", 1)]
        mine = jnp.concatenate([doubled(one, got_one, x), doubled(two, got_two, y)])
        (received,) = yield [(mine, "core", 1)]
        self.pieces = (mine, received)
        yield []


class Move:
    def __init__(self, values, kind):
        self.sends = [(values, kind, 1)]

    def put(self, received):
        (self.result,) = received
        self.sends = []


class Small:
    def __init__(self, values):
        self.steps = self.run(values)
        self.sends = next(self.steps)

    def run(self, values):
        kinds, offset = [("core", 1), ("x", 1), ("y", 1)], 1
        while 4 * offset < lax.axis_size("dp"):
            kinds.append(("z", offset))
            offset *= 2
        for kind, offset in kinds:
            (received,) = yield [(values, kind, offset)]
            values = values + received
        self.total = values
        yield []

    def put(self, received):
        self.sends = self.steps.send(received)


def beside(sums, kernel, arrays):
    sent = [[array for array, _, _ in one.sends] for one in sums]
    ways = [[(kind, offset) for _, kind, offset in one.sends] for one in sums]
    sent, arrays = lax.optimization_barrier((sent, arrays))
    got = [
        [exchange(array, *way) for array, way in zip(*each)] for each in zip(sent, ways)
    ]
    outs = kernel(*arrays) if kernel else ()
    outs, got = lax.optimization_barrier((outs, got))
    for one, received in zip(sums, got):
        one.put(received)
    return outs


def finish(place, mine, far, *outs):
    start = 0
    for out in outs:
        cols = slice(start, start + out.shape[1])
        start += out.shape[1]

        @pl.when(pl.program_id(0) == 0)
        def _(out=out, cols=cols):
            out[...] = mine[:, cols]

        @pl.when(pl.program_id(0) == 1)
        def _(out=out, cols=cols):
            out[...] = far[:, cols]


def finished(pieces, widths, name):
    rows = pieces[0].shape[0]
    place = place_of()[0].astype(jnp.int32).reshape(1)
    return call(
        finish,
        2,
        [place],
        [whole(piece) for piece in pieces],
        [
            (struct(2 * rows, w), pl.BlockSpec((rows, w), lambda i, place: (place[0] ^ i, 0)))
            for w in widths
        ],
        [],
        0,
        name,
    )


def copy_out(*refs):
    count = len(refs) // 2
    for source, target in zip(refs[:count], refs[count:]):
        target[...] = source[...]


def copied(arrays, steps):
    blocks = [
        pl.BlockSpec((array.shape[0] // steps, array.shape[1]), lambda i: (i, 0))
        for array in arrays
    ]
    return call(
        copy_out,
        steps,
        [],
        list(zip(arrays, blocks)),
        [(struct(*array.shape), block) for array, block in zip(arrays, blocks)],
        [],
        0,
        "copied",
    )


def whole_spec(shape):
    return pl.BlockSpec(shape, lambda i, *_: (0,) * len(shape))


def item_spec(shape):
    return pl.BlockSpec((1,) + shape[1:], lambda i, *_: (i,) + (0,) * (len(shape) - 1))


def own_spec(shape, items):
    return pl.BlockSpec((1,) + shape[1:], lambda i, place: (place[0] * items + i, 0, 0))


def struct(*shape):
    return jax.ShapeDtypeStruct(shape, f32)


def call(kernel, grid, prefetch, ins, outs, scratch, flops, name):
    built = pl.pallas_call(
        kernel,
        grid_spec=pltpu.PrefetchScalarGridSpec(
            num_scalar_prefetch=len(prefetch),
            grid=(grid,),
            in_specs=[spec for _, spec in ins],
            out_specs=[spec for _, spec in outs],
            scratch_shapes=scratch,
        ),
        out_shape=[out for out, _ in outs],
        compiler_params=pltpu.CompilerParams(
            dimension_semantics=("arbitrary",), vmem_limit_bytes=VMEM_LIMIT
        ),
        cost_estimate=pl.CostEstimate(flops=flops, bytes_accessed=0, transcendentals=0),
        name=name,
    )
    return built(*prefetch, *[array for array, _ in ins])


def split_scratch(*shape):
    return pltpu.VMEM((2,) + shape, bf16)


def whole(array):
    return (array, whole_spec(array.shape))


def by_item(array):
    return (array, item_spec(array.shape))


def shards(
    inputs,
    memory,
    timesteps,
    mask_flags,
    time_table,
    mask_vector,
    first_gain,
    first_bias,
    self_qkv,
    self_out,
    cross_query,
    cross_kv,
    cross_out,
    second_gain,
    second_bias,
    expand_weight,
    reduce_weight,
    cotangent,
):
    items, length, width = inputs.shape
    half = memory.shape[1]
    positions = 2 * half
    feed_width = expand_weight.shape[1]
    mac = items * length * width * width
    swap = [(0, 1), (1, 0)]
    src = lax.axis_index("src")
    place = src.astype(jnp.int32).reshape(1)

    memory_far = lax.ppermute(
        lax.dynamic_slice_in_dim(memory, (1 - src) * items, items, 0), "src", swap
    )
    chosen = mask_flags[:, None, :]
    vectors = [v[None, :] for v in (mask_vector, first_gain, first_bias, second_gain, second_bias)]
    mask_row, first_gain_row, first_bias_row, second_gain_row, second_bias_row = vectors

    def rows_out(*shape):
        return (struct(*shape), item_spec(shape))

    def whole_out(*shape):
        return (struct(*shape), whole_spec(shape))

    normed, inverse, packed, self_weights_kept, self_attended, middle, queries = call(
        self_forward,
        items,
        [timesteps],
        [
            by_item(inputs),
            by_item(chosen),
            whole(time_table),
            whole(mask_row),
            whole(first_gain_row),
            whole(first_bias_row),
            whole(self_qkv),
            whole(self_out),
            whole(cross_query),
        ],
        [
            rows_out(items, length, width),
            rows_out(items, length, 1),
            rows_out(items, length, 3 * width),
            rows_out(items, HEADS // 2, length, 2 * length),
            rows_out(items, length, width),
            rows_out(items, length, width),
            rows_out(items, length, width),
        ],
        [
            split_scratch(width, 3 * width),
            split_scratch(width, width),
            split_scratch(width, width),
        ],
        6 * 6 * mac,
        "self_forward",
    )
    memory_both, pairs, cross_weights_kept, cross_attended, after = call(
        cross_forward,
        items,
        [place],
        [
            (memory, own_spec(memory.shape, items)),
            by_item(memory_far),
            by_item(queries),
            by_item(middle),
            whole(cross_kv),
            whole(cross_out),
        ],
        [
            rows_out(items, positions, width),
            rows_out(items, positions, 2 * width),
            rows_out(items, HEADS // 2, length, 2 * positions),
            rows_out(items, length, width),
            rows_out(items, length, width),
        ],
        [split_scratch(width, 2 * width), split_scratch(width, width)],
        6 * 4 * mac,
        "cross_forward",
    )

    tokens = items * length
    after_flat = after.reshape(tokens, width)
    cot_flat = cotangent.reshape(tokens, width)

    parts = feed_width // width

    def part_of(j):
        return jnp.minimum(j, parts - 1)

    feed_cols = pl.BlockSpec((width, width), lambda j: (0, part_of(j)))
    feed_rows = pl.BlockSpec((width, width), lambda j: (part_of(j), 0))
    (
        output,
        grad_after,
        reduce_g,
        expand_g,
        cross_out_g,
        second_gain_g,
        second_bias_g,
    ) = call(
        feed,
        parts + 1,
        [],
        [
            whole(after_flat),
            whole(cot_flat),
            whole(cross_attended.reshape(tokens, width)),
            whole(second_gain_row),
            whole(second_bias_row),
            (expand_weight, feed_cols),
            (reduce_weight, feed_rows),
        ],
        [
            whole_out(tokens, width),
            whole_out(tokens, width),
            (struct(feed_width, width), feed_rows),
            (struct(width, feed_width), feed_cols),
            whole_out(width, width),
            whole_out(1, width),
            whole_out(1, width),
        ],
        [split_scratch(tokens, width), split_scratch(tokens, width)],
        6 * 25 * mac,
        "feed",
    )
    output = output.reshape(items, length, width)
    grad_after = grad_after.reshape(items, length, width)

    def backward():
        def cross_call(queries, pairs, kept, attended, grad_after):
            return call(
                cross_backward,
                items,
                [],
                [
                    by_item(queries),
                    by_item(pairs),
                    by_item(kept),
                    by_item(attended),
                    by_item(grad_after),
                    whole(cross_out),
                    whole(cross_query),
                    whole(cross_kv),
                ],
                [
                    rows_out(items, half, width),
                    rows_out(items, half, width),
                    rows_out(items, length, width),
                    rows_out(items, length, width),
                    rows_out(items, positions, 2 * width),
                ],
                [
                    split_scratch(width, width),
                    split_scratch(width, width),
                    split_scratch(width, 2 * width),
                ],
                6 * 6 * mac,
                "cross_backward",
            )

        own_grad, far_grad, grad_middle, grad_queries, grad_pairs = beside(
            [],
            cross_call,
            (queries, pairs, cross_weights_kept, cross_attended, grad_after),
        )

        def flat(values):
            return values.reshape(-1, values.shape[-1])

        def cross_weights_call(*arrays):
            pairs_spec = pl.BlockSpec((items * positions, width), lambda i: (0, jnp.clip(i - 1, 0, 1)))
            ins = [whole(flat(array)) for array in arrays]
            ins[3] = (ins[3][0], pairs_spec)
            return call(
                cross_weights,
                4,
                [],
                ins,
                [(struct(width, 4 * width), pl.BlockSpec((width, width), lambda i: (0, i)))],
                [],
                6 * 4 * mac,
                "cross_weights",
            )

        moved = Move(far_grad, "y")
        (cross_grads,) = beside(
            [],
            cross_weights_call,
            (
                middle,
                grad_queries,
                memory_both,
                grad_pairs,
                self_attended,
                grad_middle,
            ),
        )
        crossed = Sum(cross_grads)

        def self_call(packed, kept, attended, grad_middle):
            return call(
                self_backward,
                items,
                [],
                [
                    by_item(packed),
                    by_item(kept),
                    by_item(attended),
                    by_item(grad_middle),
                    whole(self_out),
                ],
                [rows_out(items, length, 3 * width)],
                [split_scratch(width, width)],
                6 * 4 * mac,
                "self_backward",
            )

        (grad_packed,) = beside(
            [crossed, moved],
            self_call,
            (packed, self_weights_kept, self_attended, grad_middle),
        )

        def self_weights_call(normed, grad_packed):
            normed, grad_packed = flat(normed), flat(grad_packed)
            return call(
                self_weights,
                3,
                [],
                [
                    whole(normed),
                    whole(first_gain_row),
                    whole(first_bias_row),
                    (grad_packed, pl.BlockSpec((tokens, width), lambda i: (0, i))),
                ],
                [(struct(width, 3 * width), pl.BlockSpec((width, width), lambda i: (0, i)))],
                [split_scratch(tokens, width)],
                6 * 3 * mac,
                "self_weights",
            )

        (self_grads,) = beside([crossed], self_weights_call, (normed, grad_packed))
        selfed = Sum(self_grads)

        def start_call(normed, inverse, chosen, grad_packed, grad_middle):
            return call(
                start_backward,
                items,
                [timesteps],
                [
                    by_item(normed),
                    by_item(inverse),
                    by_item(chosen),
                    by_item(grad_packed),
                    by_item(grad_middle),
                    whole(first_gain_row),
                    whole(self_qkv),
                ],
                [
                    rows_out(items, length, width),
                    whole_out(steps, width),
                    whole_out(1, width),
                    whole_out(1, width),
                    whole_out(1, width),
                ],
                [split_scratch(width, 3 * width)],
                6 * 3 * mac,
                "start_backward",
            )

        input_grad, time_rows, mask_g, first_gain_g, first_bias_g = beside(
            [crossed, selfed],
            start_call,
            (normed, inverse, chosen, grad_packed, grad_middle),
        )
        vectors = [mask_g, first_gain_g, first_bias_g, second_gain_g, second_bias_g]
        small = jnp.concatenate([*vectors, time_rows])
        small = Small(jnp.pad(small, ((0, -small.shape[0] % 8), (0, 0))))
        beside([selfed, crossed], None, ())
        beside([selfed, crossed, small], None, ())
        beside([selfed, crossed, small], None, ())
        crossed = End(crossed.halves)
        beside([crossed, selfed, small], None, ())
        beside([selfed, crossed, small], None, ())
        selfed = End(selfed.halves)
        crossed = beside(
            [selfed, small],
            lambda *pieces: finished(pieces, [width, 2 * width, width], "finish_cross"),
            crossed.pieces,
        )
        running = [selfed, small]
        while any(one.sends for one in running):
            beside([one for one in running if one.sends], None, ())
        (self_qkv_g,) = finished(selfed.pieces, [3 * width], "finish")
        memory_grad = lax.dynamic_update_slice_in_dim(
            jnp.zeros_like(memory), own_grad, src * items, 0
        )
        memory_grad = lax.dynamic_update_slice_in_dim(
            memory_grad, moved.result, (1 - src) * items, 0
        )
        small = small.total
        sums = [small[k] for k in range(5)]
        return (input_grad, memory_grad, small[5 : 5 + steps], *sums, *crossed, self_qkv_g)

    def nothing():
        return jax.tree.map(
            lambda out: jnp.zeros(out.shape, out.dtype), jax.eval_shape(backward)
        )

    steps = time_table.shape[0]
    reduce_g, expand_g, cross_out_g = lax.psum((reduce_g, expand_g, cross_out_g), ALL)
    (
        input_grad,
        memory_grad,
        time_g,
        mask_g,
        first_gain_g,
        first_bias_g,
        second_gain_g,
        second_bias_g,
        cross_query_g,
        cross_kv_g,
        self_out_g,
        self_qkv_g,
    ) = lax.cond(timesteps[0] >= 0, backward, nothing)
    reduce_g, expand_g, cross_out_g = copied([reduce_g, expand_g, cross_out_g], 8)
    return (
        output,
        input_grad,
        memory_grad,
        time_g,
        mask_g,
        first_gain_g,
        first_bias_g,
        self_qkv_g,
        self_out_g,
        cross_query_g,
        cross_kv_g,
        cross_out_g,
        second_gain_g,
        second_bias_g,
        expand_g,
        reduce_g,
    )


def solution(mesh):
    tokens = P(("dp", "src"), None, None)
    placed = (tokens, P("dp", "src", None), P(("dp", "src")), P(("dp", "src"), None))
    return jax.shard_map(
        shards,
        mesh=mesh,
        in_specs=placed + (P(),) * 13 + (tokens,),
        out_specs=(tokens, tokens, P("dp", "src", None)) + (P(),) * 13,
        check_vma=False,
    )
```

```python
import functools

import jax
import jax.numpy as jnp
from jax import lax
from jax.experimental import pallas as pl
from jax.experimental.pallas import tpu as pltpu
from jax.sharding import PartitionSpec as P

HEADS = 8
EPSILON = 1e-05
ALL = ("dp", "src")
f32 = jnp.float32
bf16 = jnp.bfloat16
VMEM_LIMIT = 56 * 2**20


def split(values):
    high = values.astype(bf16)
    return high, (values - high.astype(f32)).astype(bf16)


def dot(left, right, left_dim, right_dim):
    return lax.dot_general(
        left, right, (((left_dim,), (right_dim,)), ((), ())), preferred_element_type=f32
    )


def three(left, right, left_dim=1, right_dim=0):
    left_high, left_low = left
    right_high, right_low = right
    return (
        dot(left_high, right_high, left_dim, right_dim)
        + dot(left_high, right_low, left_dim, right_dim)
        + dot(left_low, right_high, left_dim, right_dim)
    )


def keep_split(ref, values):
    high, low = split(values)
    ref[0] = high
    ref[1] = low


def pair_of(ref):
    return ref[0], ref[1]


def fetch(step, pairs, sems):
    @pl.when(step == 0)
    def _():
        for k, (source, target) in enumerate(pairs):
            pltpu.make_async_copy(source, target, sems.at[k]).start()


def await_copy(source, target, sems, k):
    pltpu.make_async_copy(source, target, sems.at[k]).wait()


def upright(row):
    n = row.shape[1]
    same = lax.broadcasted_iota(jnp.int32, (n, n), 0) == lax.broadcasted_iota(jnp.int32, (n, n), 1)
    spread_row = jnp.broadcast_to(row.astype(f32), (n, n))
    return jnp.sum(jnp.where(same, spread_row, 0.0), -1, keepdims=True)


def norm(values):
    centred = values - jnp.mean(values, -1, keepdims=True)
    inverse = lax.rsqrt(jnp.mean(centred * centred, -1, keepdims=True) + EPSILON)
    return centred * inverse, inverse


def norm_back(grad_out, normed, inverse, gain):
    scaled = grad_out * gain
    return inverse * (
        scaled
        - jnp.mean(scaled, -1, keepdims=True)
        - normed * jnp.mean(scaled * normed, -1, keepdims=True)
    )


def stacked(values):
    lane = lax.broadcasted_iota(jnp.int32, values.shape, 1)
    first = lane < values.shape[1] // 2
    return split(
        jnp.concatenate([jnp.where(first, values, 0.0), jnp.where(first, 0.0, values)], 0)
    )


def scores(left, both):
    high, low = left
    both_high, both_low = both
    return dot(
        jnp.concatenate([high, low], 1), jnp.concatenate([both_high, both_high], 1), 1, 1
    ) + dot(high, both_low, 1, 1)


def spread(weights, values, dim):
    high, low = weights
    value_high, value_low = values
    both = dot(high, jnp.concatenate([value_high, value_low], 1), dim, 0)
    size = value_high.shape[1]
    return both[:, :size] + both[:, size:] + dot(low, value_high, dim, 0)


def own_lanes(values):
    n = values.shape[0] // 2
    lane = lax.broadcasted_iota(jnp.int32, (n, values.shape[1]), 1)
    return jnp.where(lane < values.shape[1] // 2, values[:n], values[n:])


def attend(queries, keys, values, weights_ref, out_ref):
    size = 2 * queries.shape[1] // HEADS
    count = keys.shape[0]
    scale = (size // 2) ** (-0.5)
    first = lax.broadcasted_iota(jnp.int32, (queries.shape[0], size), 1) < size // 2
    first_keys = lax.broadcasted_iota(jnp.int32, (count, size), 1) < size // 2
    for pair in range(HEADS // 2):
        lanes = slice(pair * size, (pair + 1) * size)
        pair_queries = queries[:, lanes] * scale
        pair_keys = split(keys[:, lanes])
        pair_values = values[:, lanes]
        total = 0.0
        for e in range(2):
            own = first if e == 0 else jnp.logical_not(first)
            own_keys = first_keys if e == 0 else jnp.logical_not(first_keys)
            score = scores(split(jnp.where(own, pair_queries, 0.0)), pair_keys)
            exponent = jnp.exp(score - jnp.max(score, -1, keepdims=True))
            weights = exponent * (1.0 / jnp.sum(exponent, -1, keepdims=True))
            weights_ref[0, pair, :, e * count : (e + 1) * count] = weights
            total = total + spread(
                split(weights), split(jnp.where(own_keys, pair_values, 0.0)), 1
            )
        out_ref[:, lanes] = total


def attend_back(queries, keys, values, weights_ref, grad, attended, put):
    size = 2 * queries.shape[1] // HEADS
    count = keys.shape[0]
    scale = (size // 2) ** (-0.5)
    first = lax.broadcasted_iota(jnp.int32, (queries.shape[0], size), 1) < size // 2
    for pair in range(HEADS // 2):
        lanes = slice(pair * size, (pair + 1) * size)
        pair_grad = grad[:, lanes]
        grad_pair = split(pair_grad)
        products = pair_grad * attended[:, lanes]
        weights = weights_ref[0, pair]
        grad_weights = scores(grad_pair, stacked(values[:, lanes]))
        parts = []
        for e in range(2):
            own = first if e == 0 else jnp.logical_not(first)
            dots = jnp.sum(jnp.where(own, products, 0.0), -1, keepdims=True)
            cols = slice(e * count, (e + 1) * count)
            parts.append(weights[:, cols] * (grad_weights[:, cols] - dots))
        grad_scores = split(jnp.concatenate(parts, 1))
        grad_queries = spread(grad_scores, stacked(keys[:, lanes]), 1)
        grad_keys = own_lanes(spread(grad_scores, split(queries[:, lanes] * scale), 0))
        grad_values = own_lanes(spread(split(weights), grad_pair, 0))
        put(lanes, grad_queries * scale, grad_keys, grad_values)


def self_forward(
    stamps,
    inputs,
    chosen,
    time_table,
    mask_vector,
    gain,
    bias,
    qkv_weight,
    out_weight,
    query_weight,
    normed_out,
    inverse_out,
    qkv_out,
    weights_out,
    attended_out,
    middle_out,
    query_out,
    qkv_split,
    out_split,
    query_split,
    out_landed,
    query_landed,
    sems,
):
    item = pl.program_id(0)
    fetch(item, [(out_weight, out_landed), (query_weight, query_landed)], sems)

    @pl.when(item == 0)
    def _():
        keep_split(qkv_split, qkv_weight[...])

    flags = upright(chosen[0])
    start = (
        inputs[0] * (1.0 - flags)
        + flags * mask_vector[...]
        + time_table[pl.ds(stamps[item], 1), :]
    )
    normed, inverse = norm(start)
    normed_out[0] = normed
    inverse_out[0] = inverse
    packed = three(split(normed * gain[...] + bias[...]), pair_of(qkv_split))
    qkv_out[0] = packed
    width = start.shape[1]
    attend(
        packed[:, :width],
        packed[:, width : 2 * width],
        packed[:, 2 * width :],
        weights_out,
        attended_out.at[0],
    )

    @pl.when(item == 0)
    def _():
        await_copy(out_weight, out_landed, sems, 0)
        keep_split(out_split, out_landed[...])
        await_copy(query_weight, query_landed, sems, 1)
        keep_split(query_split, query_landed[...])

    middle = start + three(split(attended_out[0]), pair_of(out_split))
    middle_out[0] = middle
    query_out[0] = three(split(middle), pair_of(query_split))


def cross_forward(
    place,
    memory_own,
    memory_far,
    queries,
    middle,
    kv_weight,
    out_weight,
    memory_out,
    kv_out,
    weights_out,
    attended_out,
    after_out,
    kv_split,
    out_split,
):
    @pl.when(pl.program_id(0) == 0)
    def _():
        keep_split(kv_split, kv_weight[...])
        keep_split(out_split, out_weight[...])

    memory = jnp.concatenate([memory_own[0], memory_far[0]], 0)
    memory_out[0] = memory
    pairs = three(split(memory), pair_of(kv_split))
    kv_out[0] = pairs
    width = memory.shape[1]
    attend(queries[0], pairs[:, :width], pairs[:, width:], weights_out, attended_out.at[0])
    after_out[0] = middle[0] + three(split(attended_out[0]), pair_of(out_split))


def feed(
    after,
    cotangent,
    attended,
    gain,
    bias,
    expand,
    reduce,
    output,
    grad_after,
    reduce_grad,
    expand_grad,
    out_grad,
    gain_grad,
    bias_grad,
    normed_split,
    cot_split,
    landed,
    sems,
):
    step = pl.program_id(0)
    last = pl.num_programs(0) - 1
    fetch(step, [(attended, landed)], sems)

    @pl.when(step == 0)
    def _():
        normed, _ = norm(after[...])
        keep_split(normed_split, normed * gain[...] + bias[...])
        keep_split(cot_split, cotangent[...])
        output[...] = after[...]
        grad_after[...] = jnp.zeros_like(grad_after)

    @pl.when(step < last)
    def _():
        expand_pair = split(expand[...])
        reduce_pair = split(reduce[...])
        pre = three(pair_of(normed_split), expand_pair)
        grad_hidden = three(pair_of(cot_split), reduce_pair, 1, 1)
        cdf = 0.5 * (1.0 + lax.erf(pre * (0.5**0.5)))
        slope = cdf + pre * (jnp.exp(-0.5 * pre * pre) * 0.3989422804014327)
        hidden = split(pre * cdf)
        output[...] += three(hidden, reduce_pair)
        reduce_grad[...] = three(hidden, pair_of(cot_split), 0, 0)
        grad_pre = split(grad_hidden * slope)
        expand_grad[...] = three(pair_of(normed_split), grad_pre, 0, 0)
        grad_after[...] += three(grad_pre, expand_pair, 1, 1)

    @pl.when(step == last)
    def _():
        normed, inverse = norm(after[...])
        grad = grad_after[...]
        gain_grad[...] = jnp.sum(grad * normed, 0, keepdims=True)
        bias_grad[...] = jnp.sum(grad, 0, keepdims=True)
        grad = cotangent[...] + norm_back(grad, normed, inverse, gain[...])
        grad_after[...] = grad
        await_copy(attended, landed, sems, 0)
        out_grad[...] = three(split(landed[...]), split(grad), 0, 0)


def cross_backward(
    place,
    queries,
    pairs,
    weights,
    attended,
    grad_after,
    out_weight,
    query_weight,
    kv_weight,
    own_grad,
    far_grad,
    middle_grad,
    grad_queries,
    grad_pairs,
    out_split,
    query_split,
    kv_split,
    query_landed,
    kv_landed,
    sems,
):
    item = pl.program_id(0)
    fetch(item, [(query_weight, query_landed), (kv_weight, kv_landed)], sems)

    @pl.when(item == 0)
    def _():
        keep_split(out_split, out_weight[...])

    width = queries.shape[2]
    upstream = grad_after[0]
    grad = three(split(upstream), pair_of(out_split), 1, 1)

    def put(lanes, query_part, key_part, value_part):
        grad_queries[0, :, lanes] = query_part
        grad_pairs[0, :, lanes] = key_part
        grad_pairs[0, :, lanes.start + width : lanes.stop + width] = value_part

    attend_back(
        queries[0],
        pairs[0, :, :width],
        pairs[0, :, width:],
        weights,
        grad,
        attended[0],
        put,
    )

    @pl.when(item == 0)
    def _():
        await_copy(query_weight, query_landed, sems, 0)
        keep_split(query_split, query_landed[...])
        await_copy(kv_weight, kv_landed, sems, 1)
        keep_split(kv_split, kv_landed[...])

    middle_grad[0] = upstream + three(split(grad_queries[0]), pair_of(query_split), 1, 1)
    memory_grad = three(split(grad_pairs[0]), pair_of(kv_split), 1, 1)
    half = own_grad.shape[1]
    own_grad[0] = memory_grad[:half]
    far_grad[0] = memory_grad[half:]


def cross_weights(
    middle,
    grad_queries,
    memory,
    grad_pairs,
    self_attended,
    grad_middle,
    out,
    memory_landed,
    attended_landed,
    grad_landed,
    sems,
):
    step = pl.program_id(0)
    fetch(
        step,
        [
            (memory, memory_landed),
            (self_attended, attended_landed),
            (grad_middle, grad_landed),
        ],
        sems,
    )

    def product(left, right):
        out[...] = three(split(left[...]), split(right[...]), 0, 0)

    @pl.when(step == 0)
    def _():
        product(middle, grad_queries)

    @pl.when(step == 1)
    def _():
        await_copy(memory, memory_landed, sems, 0)

    @pl.when((step == 1) | (step == 2))
    def _():
        product(memory_landed, grad_pairs)

    @pl.when(step == 3)
    def _():
        await_copy(self_attended, attended_landed, sems, 1)
        await_copy(grad_middle, grad_landed, sems, 2)
        product(attended_landed, grad_landed)


def self_backward(
    packed,
    weights,
    attended,
    grad_middle,
    out_weight,
    grad_packed,
    out_split,
):
    @pl.when(pl.program_id(0) == 0)
    def _():
        keep_split(out_split, out_weight[...])

    width = attended.shape[2]
    grad = three(split(grad_middle[0]), pair_of(out_split), 1, 1)

    def put(lanes, query_part, key_part, value_part):
        for k, part in enumerate((query_part, key_part, value_part)):
            grad_packed[0, :, lanes.start + k * width : lanes.stop + k * width] = part

    attend_back(
        packed[0, :, :width],
        packed[0, :, width : 2 * width],
        packed[0, :, 2 * width :],
        weights,
        grad,
        attended[0],
        put,
    )


def self_weights(normed, gain, bias, grad_packed, out, normed_split):
    @pl.when(pl.program_id(0) == 0)
    def _():
        keep_split(normed_split, normed[...] * gain[...] + bias[...])

    out[...] = three(pair_of(normed_split), split(grad_packed[...]), 0, 0)


def start_backward(
    stamps,
    normed,
    inverse,
    chosen,
    grad_packed,
    grad_middle,
    gain,
    qkv_weight,
    input_grad,
    time_grad,
    mask_grad,
    gain_grad,
    bias_grad,
    qkv_split,
):
    item = pl.program_id(0)

    @pl.when(item == 0)
    def _():
        keep_split(qkv_split, qkv_weight[...])
        for ref in (time_grad, mask_grad, gain_grad, bias_grad):
            ref[...] = jnp.zeros_like(ref)

    grad_normed = three(split(grad_packed[0]), pair_of(qkv_split), 1, 1)
    unit = normed[0]
    gain_grad[...] += jnp.sum(grad_normed * unit, 0, keepdims=True)
    bias_grad[...] += jnp.sum(grad_normed, 0, keepdims=True)
    grad_start = grad_middle[0] + norm_back(grad_normed, unit, inverse[0], gain[...])
    flags = upright(chosen[0])
    input_grad[0] = grad_start * (1.0 - flags)
    mask_grad[...] += jnp.sum(grad_start * flags, 0, keepdims=True)
    row = pl.ds(stamps[item], 1)
    time_grad[row, :] += jnp.sum(grad_start, 0, keepdims=True)


def exchange(values, kind, offset=1):
    groups, halves = lax.axis_size("dp"), lax.axis_size("src")
    shift = {"core": offset, "x": 2 * offset, "z": 4 * offset, "y": 0}[kind]
    pairs = []
    for d in range(groups):
        for s in range(halves):
            target = d * halves + (s ^ 1) if kind == "y" else (d ^ shift) * halves + s
            pairs.append((d * halves + s, target))
    return lax.ppermute(values, ALL, pairs)


def take(values, dim, index):
    return lax.dynamic_index_in_dim(values, index, dim, keepdims=False)


def place_of():
    group = lax.axis_index("dp")
    return group & 1, (group >> 1) & 1, lax.axis_index("src"), (group >> 2) & 3


def doubled(values, received, bit):
    return jnp.where(
        bit == 0, jnp.concatenate([values, received]), jnp.concatenate([received, values])
    )


class Sum:
    def __init__(self, values):
        self.steps = self.run(values)
        self.sends = next(self.steps)

    def run(self, values):
        core, x, y, z = place_of()
        rows, width = values.shape
        values = values.reshape(2, rows // 2, width)
        (received,) = yield [(take(values, 0, 1 - core), "core", 1)]
        values = take(values, 0, core) + received
        values = values.reshape(2, 2, 2, 4, rows // 64, width)
        one, two = values[0], values[1]
        for first, second, bit, other in (("x", "y", x, y), ("y", "x", y, x)):
            got_one, got_two = yield [
                (take(one, 0, 1 - bit), first, 1),
                (take(two, 0, 1 - other), second, 1),
            ]
            one = take(one, 0, bit) + got_one
            two = take(two, 0, other) + got_two
        both = jnp.stack([one, two])
        got = yield [(take(both, 1, z ^ k), "z", k) for k in (1, 2, 3)]
        share = take(both, 1, z) + got[0] + got[1] + got[2]
        offset = 4
        while 4 * offset < lax.axis_size("dp"):
            share = share + exchange(share, "z", offset)
            offset *= 2
        got = yield [(share, "z", k) for k in (1, 2, 3)]
        parts = [share, *got]

        def at(k):
            found = parts[0]
            for j in (1, 2, 3):
                found = jnp.where((z ^ j) == k, parts[j], found)
            return found

        both = jnp.stack([at(k) for k in range(4)], 1)
        one, two = both[0].reshape(rows // 16, width), both[1].reshape(rows // 16, width)
        got_one, got_two = yield [(one, "y", 1), (two, "x", 1)]
        self.halves = (doubled(one, got_one, y), doubled(two, got_two, x))
        yield []

    def put(self, received):
        self.sends = self.steps.send(received)


class End(Sum):
    def __init__(self, halves):
        self.steps = self.finish(*halves)
        self.sends = next(self.steps)

    def finish(self, one, two):
        _, x, y, _ = place_of()
        got_one, got_two = yield [(one, "x", 1), (two, "y", 1)]
        mine = jnp.concatenate([doubled(one, got_one, x), doubled(two, got_two, y)])
        (received,) = yield [(mine, "core", 1)]
        self.pieces = (mine, received)
        yield []


class Move:
    def __init__(self, values, kind):
        self.sends = [(values, kind, 1)]

    def put(self, received):
        (self.result,) = received
        self.sends = []


class Small:
    def __init__(self, values):
        self.steps = self.run(values)
        self.sends = next(self.steps)

    def run(self, values):
        kinds, offset = [("core", 1), ("x", 1), ("y", 1)], 1
        while 4 * offset < lax.axis_size("dp"):
            kinds.append(("z", offset))
            offset *= 2
        for kind, offset in kinds:
            (received,) = yield [(values, kind, offset)]
            values = values + received
        self.total = values
        yield []

    def put(self, received):
        self.sends = self.steps.send(received)


def beside(sums, kernel, arrays):
    sent = [[array for array, _, _ in one.sends] for one in sums]
    ways = [[(kind, offset) for _, kind, offset in one.sends] for one in sums]
    sent, arrays = lax.optimization_barrier((sent, arrays))
    got = [
        [exchange(array, *way) for array, way in zip(*each)] for each in zip(sent, ways)
    ]
    outs = kernel(*arrays) if kernel else ()
    outs, got = lax.optimization_barrier((outs, got))
    for one, received in zip(sums, got):
        one.put(received)
    return outs


def finish(place, mine, far, *outs):
    start = 0
    for out in outs:
        cols = slice(start, start + out.shape[1])
        start += out.shape[1]

        @pl.when(pl.program_id(0) == 0)
        def _(out=out, cols=cols):
            out[...] = mine[:, cols]

        @pl.when(pl.program_id(0) == 1)
        def _(out=out, cols=cols):
            out[...] = far[:, cols]


def finished(pieces, widths, name):
    rows = pieces[0].shape[0]
    place = place_of()[0].astype(jnp.int32).reshape(1)
    return call(
        finish,
        2,
        [place],
        [whole(piece) for piece in pieces],
        [
            (struct(2 * rows, w), pl.BlockSpec((rows, w), lambda i, place: (place[0] ^ i, 0)))
            for w in widths
        ],
        [],
        0,
        name,
    )


def copy_out(*refs):
    count = len(refs) // 2
    for source, target in zip(refs[:count], refs[count:]):
        target[...] = source[...]


def copied(arrays, steps):
    blocks = [
        pl.BlockSpec((array.shape[0] // steps, array.shape[1]), lambda i: (i, 0))
        for array in arrays
    ]
    return call(
        copy_out,
        steps,
        [],
        list(zip(arrays, blocks)),
        [(struct(*array.shape), block) for array, block in zip(arrays, blocks)],
        [],
        0,
        "copied",
    )


def whole_spec(shape):
    return pl.BlockSpec(shape, lambda i, *_: (0,) * len(shape))


def item_spec(shape):
    return pl.BlockSpec((1,) + shape[1:], lambda i, *_: (i,) + (0,) * (len(shape) - 1))


def own_spec(shape, items):
    return pl.BlockSpec((1,) + shape[1:], lambda i, place: (place[0] * items + i, 0, 0))


def struct(*shape):
    return jax.ShapeDtypeStruct(shape, f32)


def call(kernel, grid, prefetch, ins, outs, scratch, flops, name):
    built = pl.pallas_call(
        kernel,
        grid_spec=pltpu.PrefetchScalarGridSpec(
            num_scalar_prefetch=len(prefetch),
            grid=(grid,),
            in_specs=[spec for _, spec in ins],
            out_specs=[spec for _, spec in outs],
            scratch_shapes=scratch,
        ),
        out_shape=[out for out, _ in outs],
        compiler_params=pltpu.CompilerParams(
            dimension_semantics=("arbitrary",), vmem_limit_bytes=VMEM_LIMIT
        ),
        cost_estimate=pl.CostEstimate(flops=flops, bytes_accessed=0, transcendentals=0),
        name=name,
    )
    return built(*prefetch, *[array for array, _ in ins])


def split_scratch(*shape):
    return pltpu.VMEM((2,) + shape, bf16)


def whole(array):
    return (array, whole_spec(array.shape))


def later(array):
    return (array, pl.BlockSpec(memory_space=pl.ANY))


def landing(*shape):
    return pltpu.VMEM(shape, f32)


def copies(count):
    return pltpu.SemaphoreType.DMA((count,))


def by_item(array):
    return (array, item_spec(array.shape))


def shards(
    inputs,
    memory,
    timesteps,
    mask_flags,
    time_table,
    mask_vector,
    first_gain,
    first_bias,
    self_qkv,
    self_out,
    cross_query,
    cross_kv,
    cross_out,
    second_gain,
    second_bias,
    expand_weight,
    reduce_weight,
    cotangent,
):
    items, length, width = inputs.shape
    half = memory.shape[1]
    positions = 2 * half
    feed_width = expand_weight.shape[1]
    mac = items * length * width * width
    swap = [(0, 1), (1, 0)]
    src = lax.axis_index("src")
    place = src.astype(jnp.int32).reshape(1)

    memory_far = lax.ppermute(
        lax.dynamic_slice_in_dim(memory, (1 - src) * items, items, 0), "src", swap
    )
    chosen = mask_flags[:, None, :]
    vectors = [v[None, :] for v in (mask_vector, first_gain, first_bias, second_gain, second_bias)]
    mask_row, first_gain_row, first_bias_row, second_gain_row, second_bias_row = vectors

    def rows_out(*shape):
        return (struct(*shape), item_spec(shape))

    def whole_out(*shape):
        return (struct(*shape), whole_spec(shape))

    normed, inverse, packed, self_weights_kept, self_attended, middle, queries = call(
        self_forward,
        items,
        [timesteps],
        [
            by_item(inputs),
            by_item(chosen),
            whole(time_table),
            whole(mask_row),
            whole(first_gain_row),
            whole(first_bias_row),
            whole(self_qkv),
            later(self_out),
            later(cross_query),
        ],
        [
            rows_out(items, length, width),
            rows_out(items, length, 1),
            rows_out(items, length, 3 * width),
            rows_out(items, HEADS // 2, length, 2 * length),
            rows_out(items, length, width),
            rows_out(items, length, width),
            rows_out(items, length, width),
        ],
        [
            split_scratch(width, 3 * width),
            split_scratch(width, width),
            split_scratch(width, width),
            landing(width, width),
            landing(width, width),
            copies(2),
        ],
        6 * 6 * mac,
        "self_forward",
    )
    memory_both, pairs, cross_weights_kept, cross_attended, after = call(
        cross_forward,
        items,
        [place],
        [
            (memory, own_spec(memory.shape, items)),
            by_item(memory_far),
            by_item(queries),
            by_item(middle),
            whole(cross_kv),
            whole(cross_out),
        ],
        [
            rows_out(items, positions, width),
            rows_out(items, positions, 2 * width),
            rows_out(items, HEADS // 2, length, 2 * positions),
            rows_out(items, length, width),
            rows_out(items, length, width),
        ],
        [split_scratch(width, 2 * width), split_scratch(width, width)],
        6 * 4 * mac,
        "cross_forward",
    )

    tokens = items * length
    after_flat = after.reshape(tokens, width)
    cot_flat = cotangent.reshape(tokens, width)

    parts = feed_width // width

    def part_of(j):
        return jnp.minimum(j, parts - 1)

    feed_cols = pl.BlockSpec((width, width), lambda j: (0, part_of(j)))
    feed_rows = pl.BlockSpec((width, width), lambda j: (part_of(j), 0))
    (
        output,
        grad_after,
        reduce_g,
        expand_g,
        cross_out_g,
        second_gain_g,
        second_bias_g,
    ) = call(
        feed,
        parts + 1,
        [],
        [
            whole(after_flat),
            whole(cot_flat),
            later(cross_attended.reshape(tokens, width)),
            whole(second_gain_row),
            whole(second_bias_row),
            (expand_weight, feed_cols),
            (reduce_weight, feed_rows),
        ],
        [
            whole_out(tokens, width),
            whole_out(tokens, width),
            (struct(feed_width, width), feed_rows),
            (struct(width, feed_width), feed_cols),
            whole_out(width, width),
            whole_out(1, width),
            whole_out(1, width),
        ],
        [
            split_scratch(tokens, width),
            split_scratch(tokens, width),
            landing(tokens, width),
            copies(1),
        ],
        6 * 25 * mac,
        "feed",
    )
    output = output.reshape(items, length, width)
    grad_after = grad_after.reshape(items, length, width)

    def backward():
        def cross_call(queries, pairs, kept, attended, grad_after):
            return call(
                cross_backward,
                items,
                [place],
                [
                    by_item(queries),
                    by_item(pairs),
                    by_item(kept),
                    by_item(attended),
                    by_item(grad_after),
                    whole(cross_out),
                    later(cross_query),
                    later(cross_kv),
                ],
                [
                    (struct(*memory.shape), own_spec(memory.shape, items)),
                    rows_out(items, half, width),
                    rows_out(items, length, width),
                    rows_out(items, length, width),
                    rows_out(items, positions, 2 * width),
                ],
                [
                    split_scratch(width, width),
                    split_scratch(width, width),
                    split_scratch(width, 2 * width),
                    landing(width, width),
                    landing(width, 2 * width),
                    copies(2),
                ],
                6 * 6 * mac,
                "cross_backward",
            )

        own_grad, far_grad, grad_middle, grad_queries, grad_pairs = beside(
            [],
            cross_call,
            (queries, pairs, cross_weights_kept, cross_attended, grad_after),
        )

        def flat(values):
            return values.reshape(-1, values.shape[-1])

        def cross_weights_call(*arrays):
            pairs_spec = pl.BlockSpec((items * positions, width), lambda i: (0, jnp.clip(i - 1, 0, 1)))
            ins = [whole(flat(array)) for array in arrays]
            ins[3] = (ins[3][0], pairs_spec)
            for k in (2, 4, 5):
                ins[k] = later(ins[k][0])
            return call(
                cross_weights,
                4,
                [],
                ins,
                [(struct(width, 4 * width), pl.BlockSpec((width, width), lambda i: (0, i)))],
                [
                    landing(items * positions, width),
                    landing(tokens, width),
                    landing(tokens, width),
                    copies(3),
                ],
                6 * 4 * mac,
                "cross_weights",
            )

        moved = Move(far_grad, "y")
        (cross_grads,) = beside(
            [],
            cross_weights_call,
            (
                middle,
                grad_queries,
                memory_both,
                grad_pairs,
                self_attended,
                grad_middle,
            ),
        )
        crossed = Sum(cross_grads)

        def self_call(packed, kept, attended, grad_middle):
            return call(
                self_backward,
                items,
                [],
                [
                    by_item(packed),
                    by_item(kept),
                    by_item(attended),
                    by_item(grad_middle),
                    whole(self_out),
                ],
                [rows_out(items, length, 3 * width)],
                [split_scratch(width, width)],
                6 * 4 * mac,
                "self_backward",
            )

        (grad_packed,) = beside(
            [crossed, moved],
            self_call,
            (packed, self_weights_kept, self_attended, grad_middle),
        )

        def self_weights_call(normed, grad_packed):
            normed, grad_packed = flat(normed), flat(grad_packed)
            return call(
                self_weights,
                3,
                [],
                [
                    whole(normed),
                    whole(first_gain_row),
                    whole(first_bias_row),
                    (grad_packed, pl.BlockSpec((tokens, width), lambda i: (0, i))),
                ],
                [(struct(width, 3 * width), pl.BlockSpec((width, width), lambda i: (0, i)))],
                [split_scratch(tokens, width)],
                6 * 3 * mac,
                "self_weights",
            )

        (self_grads,) = beside([crossed], self_weights_call, (normed, grad_packed))
        selfed = Sum(self_grads)

        def start_call(normed, inverse, chosen, grad_packed, grad_middle):
            return call(
                start_backward,
                items,
                [timesteps],
                [
                    by_item(normed),
                    by_item(inverse),
                    by_item(chosen),
                    by_item(grad_packed),
                    by_item(grad_middle),
                    whole(first_gain_row),
                    whole(self_qkv),
                ],
                [
                    rows_out(items, length, width),
                    whole_out(steps, width),
                    whole_out(1, width),
                    whole_out(1, width),
                    whole_out(1, width),
                ],
                [split_scratch(width, 3 * width)],
                6 * 3 * mac,
                "start_backward",
            )

        input_grad, time_rows, mask_g, first_gain_g, first_bias_g = beside(
            [crossed, selfed],
            start_call,
            (normed, inverse, chosen, grad_packed, grad_middle),
        )
        vectors = [mask_g, first_gain_g, first_bias_g, second_gain_g, second_bias_g]
        small = jnp.concatenate([*vectors, time_rows])
        small = Small(jnp.pad(small, ((0, -small.shape[0] % 8), (0, 0))))
        beside([selfed, crossed], None, ())
        beside([selfed, crossed, small], None, ())
        beside([selfed, crossed, small], None, ())
        crossed = End(crossed.halves)
        beside([crossed, selfed, small], None, ())
        beside([selfed, crossed, small], None, ())
        selfed = End(selfed.halves)
        crossed = beside(
            [selfed, small],
            lambda *pieces: finished(pieces, [width, 2 * width, width], "finish_cross"),
            crossed.pieces,
        )
        running = [selfed, small]
        while any(one.sends for one in running):
            beside([one for one in running if one.sends], None, ())
        (self_qkv_g,) = finished(selfed.pieces, [3 * width], "finish")
        memory_grad = lax.dynamic_update_slice_in_dim(
            own_grad, moved.result, (1 - src) * items, 0
        )
        small = small.total
        sums = [small[k] for k in range(5)]
        return (input_grad, memory_grad, small[5 : 5 + steps], *sums, *crossed, self_qkv_g)

    def nothing():
        return jax.tree.map(
            lambda out: jnp.zeros(out.shape, out.dtype), jax.eval_shape(backward)
        )

    steps = time_table.shape[0]
    reduce_g, expand_g, cross_out_g = lax.psum((reduce_g, expand_g, cross_out_g), ALL)
    (
        input_grad,
        memory_grad,
        time_g,
        mask_g,
        first_gain_g,
        first_bias_g,
        second_gain_g,
        second_bias_g,
        cross_query_g,
        cross_kv_g,
        self_out_g,
        self_qkv_g,
    ) = lax.cond(timesteps[0] >= 0, backward, nothing)
    reduce_g, expand_g, cross_out_g = copied([reduce_g, expand_g, cross_out_g], 2)
    return (
        output,
        input_grad,
        memory_grad,
        time_g,
        mask_g,
        first_gain_g,
        first_bias_g,
        self_qkv_g,
        self_out_g,
        cross_query_g,
        cross_kv_g,
        cross_out_g,
        second_gain_g,
        second_bias_g,
        expand_g,
        reduce_g,
    )


def solution(mesh):
    tokens = P(("dp", "src"), None, None)
    placed = (tokens, P("dp", "src", None), P(("dp", "src")), P(("dp", "src"), None))
    return jax.shard_map(
        shards,
        mesh=mesh,
        in_specs=placed + (P(),) * 13 + (tokens,),
        out_specs=(tokens, tokens, P("dp", "src", None)) + (P(),) * 13,
        check_vma=False,
    )
```

```python
import functools

import jax
import jax.numpy as jnp
from jax import lax
from jax.experimental import pallas as pl
from jax.experimental.pallas import tpu as pltpu
from jax.sharding import PartitionSpec as P

HEADS = 8
EPSILON = 1e-05
ALL = ("dp", "src")
f32 = jnp.float32
bf16 = jnp.bfloat16
VMEM_LIMIT = 56 * 2**20


def split(values):
    high = values.astype(bf16)
    return high, (values - high.astype(f32)).astype(bf16)


def dot(left, right, left_dim, right_dim):
    return lax.dot_general(
        left, right, (((left_dim,), (right_dim,)), ((), ())), preferred_element_type=f32
    )


def three(left, right, left_dim=1, right_dim=0):
    left_high, left_low = left
    right_high, right_low = right
    return (
        dot(left_high, right_high, left_dim, right_dim)
        + dot(left_high, right_low, left_dim, right_dim)
        + dot(left_low, right_high, left_dim, right_dim)
    )


def keep_split(ref, values):
    high, low = split(values)
    ref[0] = high
    ref[1] = low


def pair_of(ref):
    return ref[0], ref[1]


def fetch(step, pairs, sems):
    @pl.when(step == 0)
    def _():
        for k, (source, target) in enumerate(pairs):
            pltpu.make_async_copy(source, target, sems.at[k]).start()


def await_copy(source, target, sems, k):
    pltpu.make_async_copy(source, target, sems.at[k]).wait()


def upright(row):
    n = row.shape[1]
    same = lax.broadcasted_iota(jnp.int32, (n, n), 0) == lax.broadcasted_iota(jnp.int32, (n, n), 1)
    spread_row = jnp.broadcast_to(row.astype(f32), (n, n))
    return jnp.sum(jnp.where(same, spread_row, 0.0), -1, keepdims=True)


def norm(values):
    centred = values - jnp.mean(values, -1, keepdims=True)
    inverse = lax.rsqrt(jnp.mean(centred * centred, -1, keepdims=True) + EPSILON)
    return centred * inverse, inverse


def norm_back(grad_out, normed, inverse, gain):
    scaled = grad_out * gain
    return inverse * (
        scaled
        - jnp.mean(scaled, -1, keepdims=True)
        - normed * jnp.mean(scaled * normed, -1, keepdims=True)
    )


def stacked(values):
    lane = lax.broadcasted_iota(jnp.int32, values.shape, 1)
    first = lane < values.shape[1] // 2
    return split(
        jnp.concatenate([jnp.where(first, values, 0.0), jnp.where(first, 0.0, values)], 0)
    )


def scores(left, both):
    high, low = left
    both_high, both_low = both
    return dot(
        jnp.concatenate([high, low], 1), jnp.concatenate([both_high, both_high], 1), 1, 1
    ) + dot(high, both_low, 1, 1)


def spread(weights, values, dim):
    high, low = weights
    value_high, value_low = values
    both = dot(high, jnp.concatenate([value_high, value_low], 1), dim, 0)
    size = value_high.shape[1]
    return both[:, :size] + both[:, size:] + dot(low, value_high, dim, 0)


def own_lanes(values):
    n = values.shape[0] // 2
    lane = lax.broadcasted_iota(jnp.int32, (n, values.shape[1]), 1)
    return jnp.where(lane < values.shape[1] // 2, values[:n], values[n:])


def attend(queries, keys, values, weights_ref, out_ref):
    size = 2 * queries.shape[1] // HEADS
    count = keys.shape[0]
    scale = (size // 2) ** (-0.5)
    first = lax.broadcasted_iota(jnp.int32, (queries.shape[0], size), 1) < size // 2
    first_keys = lax.broadcasted_iota(jnp.int32, (count, size), 1) < size // 2
    for pair in range(HEADS // 2):
        lanes = slice(pair * size, (pair + 1) * size)
        pair_queries = queries[:, lanes] * scale
        pair_keys = split(keys[:, lanes])
        pair_values = values[:, lanes]
        total = 0.0
        for e in range(2):
            own = first if e == 0 else jnp.logical_not(first)
            own_keys = first_keys if e == 0 else jnp.logical_not(first_keys)
            score = scores(split(jnp.where(own, pair_queries, 0.0)), pair_keys)
            exponent = jnp.exp(score - jnp.max(score, -1, keepdims=True))
            weights = exponent * (1.0 / jnp.sum(exponent, -1, keepdims=True))
            weights_ref[0, pair, :, e * count : (e + 1) * count] = weights
            total = total + spread(
                split(weights), split(jnp.where(own_keys, pair_values, 0.0)), 1
            )
        out_ref[:, lanes] = total


def attend_back(queries, keys, values, weights_ref, grad, attended, put):
    size = 2 * queries.shape[1] // HEADS
    count = keys.shape[0]
    scale = (size // 2) ** (-0.5)
    first = lax.broadcasted_iota(jnp.int32, (queries.shape[0], size), 1) < size // 2
    for pair in range(HEADS // 2):
        lanes = slice(pair * size, (pair + 1) * size)
        pair_grad = grad[:, lanes]
        grad_pair = split(pair_grad)
        products = pair_grad * attended[:, lanes]
        weights = weights_ref[0, pair]
        grad_weights = scores(grad_pair, stacked(values[:, lanes]))
        parts = []
        for e in range(2):
            own = first if e == 0 else jnp.logical_not(first)
            dots = jnp.sum(jnp.where(own, products, 0.0), -1, keepdims=True)
            cols = slice(e * count, (e + 1) * count)
            parts.append(weights[:, cols] * (grad_weights[:, cols] - dots))
        grad_scores = split(jnp.concatenate(parts, 1))
        grad_queries = spread(grad_scores, stacked(keys[:, lanes]), 1)
        grad_keys = own_lanes(spread(grad_scores, split(queries[:, lanes] * scale), 0))
        grad_values = own_lanes(spread(split(weights), grad_pair, 0))
        put(lanes, grad_queries * scale, grad_keys, grad_values)


def self_forward(
    stamps,
    inputs,
    chosen,
    time_table,
    mask_vector,
    gain,
    bias,
    qkv_weight,
    out_weight,
    query_weight,
    normed_out,
    inverse_out,
    qkv_out,
    weights_out,
    attended_out,
    middle_out,
    query_out,
    qkv_split,
    out_split,
    query_split,
    out_landed,
    query_landed,
    sems,
):
    item = pl.program_id(0)
    fetch(item, [(out_weight, out_landed), (query_weight, query_landed)], sems)

    @pl.when(item == 0)
    def _():
        keep_split(qkv_split, qkv_weight[...])

    flags = upright(chosen[0])
    start = (
        inputs[0] * (1.0 - flags)
        + flags * mask_vector[...]
        + time_table[pl.ds(stamps[item], 1), :]
    )
    normed, inverse = norm(start)
    normed_out[0] = normed
    inverse_out[0] = inverse
    packed = three(split(normed * gain[...] + bias[...]), pair_of(qkv_split))
    qkv_out[0] = packed
    width = start.shape[1]
    attend(
        packed[:, :width],
        packed[:, width : 2 * width],
        packed[:, 2 * width :],
        weights_out,
        attended_out.at[0],
    )

    @pl.when(item == 0)
    def _():
        await_copy(out_weight, out_landed, sems, 0)
        keep_split(out_split, out_landed[...])
        await_copy(query_weight, query_landed, sems, 1)
        keep_split(query_split, query_landed[...])

    middle = start + three(split(attended_out[0]), pair_of(out_split))
    middle_out[0] = middle
    query_out[0] = three(split(middle), pair_of(query_split))


def cross_forward(
    place,
    memory_own,
    memory_far,
    queries,
    middle,
    kv_weight,
    out_weight,
    memory_out,
    kv_out,
    weights_out,
    attended_out,
    after_out,
    kv_split,
    out_split,
):
    @pl.when(pl.program_id(0) == 0)
    def _():
        keep_split(kv_split, kv_weight[...])
        keep_split(out_split, out_weight[...])

    memory = jnp.concatenate([memory_own[0], memory_far[0]], 0)
    memory_out[0] = memory
    pairs = three(split(memory), pair_of(kv_split))
    kv_out[0] = pairs
    width = memory.shape[1]
    attend(queries[0], pairs[:, :width], pairs[:, width:], weights_out, attended_out.at[0])
    after_out[0] = middle[0] + three(split(attended_out[0]), pair_of(out_split))


def feed(
    after,
    cotangent,
    attended,
    gain,
    bias,
    expand,
    reduce,
    hidden_out,
    grad_after,
    reduce_grad,
    expand_grad,
    out_grad,
    gain_grad,
    bias_grad,
    normed_split,
    cot_split,
    landed,
    sems,
):
    step = pl.program_id(0)
    last = pl.num_programs(0) - 1
    fetch(step, [(attended, landed)], sems)

    @pl.when(step == 0)
    def _():
        normed, _ = norm(after[...])
        keep_split(normed_split, normed * gain[...] + bias[...])
        keep_split(cot_split, cotangent[...])
        grad_after[...] = jnp.zeros_like(grad_after)

    @pl.when(step < last)
    def _():
        expand_pair = split(expand[...])
        reduce_pair = split(reduce[...])
        pre = three(pair_of(normed_split), expand_pair)
        grad_hidden = three(pair_of(cot_split), reduce_pair, 1, 1)
        cdf = 0.5 * (1.0 + lax.erf(pre * (0.5**0.5)))
        slope = cdf + pre * (jnp.exp(-0.5 * pre * pre) * 0.3989422804014327)
        active = pre * cdf
        hidden_out[...] = active
        hidden = split(active)
        reduce_grad[...] = three(hidden, pair_of(cot_split), 0, 0)
        grad_pre = split(grad_hidden * slope)
        expand_grad[...] = three(pair_of(normed_split), grad_pre, 0, 0)
        grad_after[...] += three(grad_pre, expand_pair, 1, 1)

    @pl.when(step == last)
    def _():
        normed, inverse = norm(after[...])
        grad = grad_after[...]
        gain_grad[...] = jnp.sum(grad * normed, 0, keepdims=True)
        bias_grad[...] = jnp.sum(grad, 0, keepdims=True)
        grad = cotangent[...] + norm_back(grad, normed, inverse, gain[...])
        grad_after[...] = grad
        await_copy(attended, landed, sems, 0)
        out_grad[...] = three(split(landed[...]), split(grad), 0, 0)


def feed_output(after, hidden, reduce, output):
    @pl.when(pl.program_id(0) == 0)
    def _():
        output[...] = after[...]

    output[...] += three(split(hidden[...]), split(reduce[...]))


def cross_backward(
    place,
    queries,
    pairs,
    weights,
    attended,
    grad_after,
    out_weight,
    query_weight,
    kv_weight,
    own_grad,
    far_grad,
    middle_grad,
    grad_queries,
    grad_pairs,
    out_split,
    query_split,
    kv_split,
    query_landed,
    kv_landed,
    sems,
):
    item = pl.program_id(0)
    fetch(item, [(query_weight, query_landed), (kv_weight, kv_landed)], sems)

    @pl.when(item == 0)
    def _():
        keep_split(out_split, out_weight[...])

    width = queries.shape[2]
    upstream = grad_after[0]
    grad = three(split(upstream), pair_of(out_split), 1, 1)

    def put(lanes, query_part, key_part, value_part):
        grad_queries[0, :, lanes] = query_part
        grad_pairs[0, :, lanes] = key_part
        grad_pairs[0, :, lanes.start + width : lanes.stop + width] = value_part

    attend_back(
        queries[0],
        pairs[0, :, :width],
        pairs[0, :, width:],
        weights,
        grad,
        attended[0],
        put,
    )

    @pl.when(item == 0)
    def _():
        await_copy(query_weight, query_landed, sems, 0)
        keep_split(query_split, query_landed[...])
        await_copy(kv_weight, kv_landed, sems, 1)
        keep_split(kv_split, kv_landed[...])

    middle_grad[0] = upstream + three(split(grad_queries[0]), pair_of(query_split), 1, 1)
    memory_grad = three(split(grad_pairs[0]), pair_of(kv_split), 1, 1)
    half = own_grad.shape[1]
    own_grad[0] = memory_grad[:half]
    far_grad[0] = memory_grad[half:]


def cross_weights(
    middle,
    grad_queries,
    memory,
    grad_pairs,
    self_attended,
    grad_middle,
    out,
    memory_landed,
    attended_landed,
    grad_landed,
    sems,
):
    step = pl.program_id(0)
    fetch(
        step,
        [
            (memory, memory_landed),
            (self_attended, attended_landed),
            (grad_middle, grad_landed),
        ],
        sems,
    )

    def product(left, right):
        out[...] = three(split(left[...]), split(right[...]), 0, 0)

    @pl.when(step == 0)
    def _():
        product(middle, grad_queries)

    @pl.when(step == 1)
    def _():
        await_copy(memory, memory_landed, sems, 0)

    @pl.when((step == 1) | (step == 2))
    def _():
        product(memory_landed, grad_pairs)

    @pl.when(step == 3)
    def _():
        await_copy(self_attended, attended_landed, sems, 1)
        await_copy(grad_middle, grad_landed, sems, 2)
        product(attended_landed, grad_landed)


def self_backward(
    packed,
    weights,
    attended,
    grad_middle,
    out_weight,
    grad_packed,
    out_split,
):
    @pl.when(pl.program_id(0) == 0)
    def _():
        keep_split(out_split, out_weight[...])

    width = attended.shape[2]
    grad = three(split(grad_middle[0]), pair_of(out_split), 1, 1)

    def put(lanes, query_part, key_part, value_part):
        for k, part in enumerate((query_part, key_part, value_part)):
            grad_packed[0, :, lanes.start + k * width : lanes.stop + k * width] = part

    attend_back(
        packed[0, :, :width],
        packed[0, :, width : 2 * width],
        packed[0, :, 2 * width :],
        weights,
        grad,
        attended[0],
        put,
    )


def self_weights(normed, gain, bias, grad_packed, out, normed_split):
    @pl.when(pl.program_id(0) == 0)
    def _():
        keep_split(normed_split, normed[...] * gain[...] + bias[...])

    out[...] = three(pair_of(normed_split), split(grad_packed[...]), 0, 0)


def start_backward(
    stamps,
    normed,
    inverse,
    chosen,
    grad_packed,
    grad_middle,
    gain,
    qkv_weight,
    input_grad,
    time_grad,
    mask_grad,
    gain_grad,
    bias_grad,
    qkv_split,
):
    item = pl.program_id(0)

    @pl.when(item == 0)
    def _():
        keep_split(qkv_split, qkv_weight[...])
        for ref in (time_grad, mask_grad, gain_grad, bias_grad):
            ref[...] = jnp.zeros_like(ref)

    grad_normed = three(split(grad_packed[0]), pair_of(qkv_split), 1, 1)
    unit = normed[0]
    gain_grad[...] += jnp.sum(grad_normed * unit, 0, keepdims=True)
    bias_grad[...] += jnp.sum(grad_normed, 0, keepdims=True)
    grad_start = grad_middle[0] + norm_back(grad_normed, unit, inverse[0], gain[...])
    flags = upright(chosen[0])
    input_grad[0] = grad_start * (1.0 - flags)
    mask_grad[...] += jnp.sum(grad_start * flags, 0, keepdims=True)
    row = pl.ds(stamps[item], 1)
    time_grad[row, :] += jnp.sum(grad_start, 0, keepdims=True)


def exchange(values, kind, offset=1):
    groups, halves = lax.axis_size("dp"), lax.axis_size("src")
    shift = {"core": offset, "x": 2 * offset, "z": 4 * offset, "y": 0}[kind]
    pairs = []
    for d in range(groups):
        for s in range(halves):
            target = d * halves + (s ^ 1) if kind == "y" else (d ^ shift) * halves + s
            pairs.append((d * halves + s, target))
    return lax.ppermute(values, ALL, pairs)


def take(values, dim, index):
    return lax.dynamic_index_in_dim(values, index, dim, keepdims=False)


def place_of():
    group = lax.axis_index("dp")
    return group & 1, (group >> 1) & 1, lax.axis_index("src"), (group >> 2) & 3


def doubled(values, received, bit):
    return jnp.where(
        bit == 0, jnp.concatenate([values, received]), jnp.concatenate([received, values])
    )


class Sum:
    def __init__(self, values):
        self.steps = self.run(values)
        self.sends = next(self.steps)

    def run(self, values):
        core, x, y, z = place_of()
        rows, width = values.shape
        values = values.reshape(2, rows // 2, width)
        (received,) = yield [(take(values, 0, 1 - core), "core", 1)]
        values = take(values, 0, core) + received
        values = values.reshape(2, 2, 2, 4, rows // 64, width)
        one, two = values[0], values[1]
        for first, second, bit, other in (("x", "y", x, y), ("y", "x", y, x)):
            got_one, got_two = yield [
                (take(one, 0, 1 - bit), first, 1),
                (take(two, 0, 1 - other), second, 1),
            ]
            one = take(one, 0, bit) + got_one
            two = take(two, 0, other) + got_two
        both = jnp.stack([one, two])
        got = yield [(take(both, 1, z ^ k), "z", k) for k in (1, 2, 3)]
        share = take(both, 1, z) + got[0] + got[1] + got[2]
        offset = 4
        while 4 * offset < lax.axis_size("dp"):
            share = share + exchange(share, "z", offset)
            offset *= 2
        got = yield [(share, "z", k) for k in (1, 2, 3)]
        parts = [share, *got]

        def at(k):
            found = parts[0]
            for j in (1, 2, 3):
                found = jnp.where((z ^ j) == k, parts[j], found)
            return found

        both = jnp.stack([at(k) for k in range(4)], 1)
        one, two = both[0].reshape(rows // 16, width), both[1].reshape(rows // 16, width)
        got_one, got_two = yield [(one, "y", 1), (two, "x", 1)]
        self.halves = (doubled(one, got_one, y), doubled(two, got_two, x))
        yield []

    def put(self, received):
        self.sends = self.steps.send(received)


class End(Sum):
    def __init__(self, halves):
        self.steps = self.finish(*halves)
        self.sends = next(self.steps)

    def finish(self, one, two):
        _, x, y, _ = place_of()
        got_one, got_two = yield [(one, "x", 1), (two, "y", 1)]
        mine = jnp.concatenate([doubled(one, got_one, x), doubled(two, got_two, y)])
        (received,) = yield [(mine, "core", 1)]
        self.pieces = (mine, received)
        yield []


class Move:
    def __init__(self, values, kind):
        self.sends = [(values, kind, 1)]

    def put(self, received):
        (self.result,) = received
        self.sends = []


class Small:
    def __init__(self, values):
        self.steps = self.run(values)
        self.sends = next(self.steps)

    def run(self, values):
        kinds, offset = [("core", 1), ("x", 1), ("y", 1)], 1
        while 4 * offset < lax.axis_size("dp"):
            kinds.append(("z", offset))
            offset *= 2
        for kind, offset in kinds:
            (received,) = yield [(values, kind, offset)]
            values = values + received
        self.total = values
        yield []

    def put(self, received):
        self.sends = self.steps.send(received)


def beside(sums, kernel, arrays):
    sent = [[array for array, _, _ in one.sends] for one in sums]
    ways = [[(kind, offset) for _, kind, offset in one.sends] for one in sums]
    sent, arrays = lax.optimization_barrier((sent, arrays))
    got = [
        [exchange(array, *way) for array, way in zip(*each)] for each in zip(sent, ways)
    ]
    outs = kernel(*arrays) if kernel else ()
    outs, got = lax.optimization_barrier((outs, got))
    for one, received in zip(sums, got):
        one.put(received)
    return outs


def finish(place, mine, far, *outs):
    start = 0
    for out in outs:
        cols = slice(start, start + out.shape[1])
        start += out.shape[1]

        @pl.when(pl.program_id(0) == 0)
        def _(out=out, cols=cols):
            out[...] = mine[:, cols]

        @pl.when(pl.program_id(0) == 1)
        def _(out=out, cols=cols):
            out[...] = far[:, cols]


def finished(pieces, widths, name):
    rows = pieces[0].shape[0]
    place = place_of()[0].astype(jnp.int32).reshape(1)
    return call(
        finish,
        2,
        [place],
        [whole(piece) for piece in pieces],
        [
            (struct(2 * rows, w), pl.BlockSpec((rows, w), lambda i, place: (place[0] ^ i, 0)))
            for w in widths
        ],
        [],
        0,
        name,
    )


def copy_out(*refs):
    count = len(refs) // 2
    for source, target in zip(refs[:count], refs[count:]):
        target[...] = source[...]


def copied(arrays, steps):
    blocks = [
        pl.BlockSpec((array.shape[0] // steps, array.shape[1]), lambda i: (i, 0))
        for array in arrays
    ]
    return call(
        copy_out,
        steps,
        [],
        list(zip(arrays, blocks)),
        [(struct(*array.shape), block) for array, block in zip(arrays, blocks)],
        [],
        0,
        "copied",
    )


def whole_spec(shape):
    return pl.BlockSpec(shape, lambda i, *_: (0,) * len(shape))


def item_spec(shape):
    return pl.BlockSpec((1,) + shape[1:], lambda i, *_: (i,) + (0,) * (len(shape) - 1))


def own_spec(shape, items):
    return pl.BlockSpec((1,) + shape[1:], lambda i, place: (place[0] * items + i, 0, 0))


def struct(*shape):
    return jax.ShapeDtypeStruct(shape, f32)


def call(kernel, grid, prefetch, ins, outs, scratch, flops, name):
    built = pl.pallas_call(
        kernel,
        grid_spec=pltpu.PrefetchScalarGridSpec(
            num_scalar_prefetch=len(prefetch),
            grid=(grid,),
            in_specs=[spec for _, spec in ins],
            out_specs=[spec for _, spec in outs],
            scratch_shapes=scratch,
        ),
        out_shape=[out for out, _ in outs],
        compiler_params=pltpu.CompilerParams(
            dimension_semantics=("arbitrary",), vmem_limit_bytes=VMEM_LIMIT
        ),
        cost_estimate=pl.CostEstimate(flops=flops, bytes_accessed=0, transcendentals=0),
        name=name,
    )
    return built(*prefetch, *[array for array, _ in ins])


def split_scratch(*shape):
    return pltpu.VMEM((2,) + shape, bf16)


def whole(array):
    return (array, whole_spec(array.shape))


def later(array):
    return (array, pl.BlockSpec(memory_space=pl.ANY))


def landing(*shape):
    return pltpu.VMEM(shape, f32)


def copies(count):
    return pltpu.SemaphoreType.DMA((count,))


def by_item(array):
    return (array, item_spec(array.shape))


def shards(
    inputs,
    memory,
    timesteps,
    mask_flags,
    time_table,
    mask_vector,
    first_gain,
    first_bias,
    self_qkv,
    self_out,
    cross_query,
    cross_kv,
    cross_out,
    second_gain,
    second_bias,
    expand_weight,
    reduce_weight,
    cotangent,
):
    items, length, width = inputs.shape
    half = memory.shape[1]
    positions = 2 * half
    feed_width = expand_weight.shape[1]
    mac = items * length * width * width
    swap = [(0, 1), (1, 0)]
    src = lax.axis_index("src")
    place = src.astype(jnp.int32).reshape(1)

    memory_far = lax.ppermute(
        lax.dynamic_slice_in_dim(memory, (1 - src) * items, items, 0), "src", swap
    )
    chosen = mask_flags[:, None, :]
    vectors = [v[None, :] for v in (mask_vector, first_gain, first_bias, second_gain, second_bias)]
    mask_row, first_gain_row, first_bias_row, second_gain_row, second_bias_row = vectors

    def rows_out(*shape):
        return (struct(*shape), item_spec(shape))

    def whole_out(*shape):
        return (struct(*shape), whole_spec(shape))

    normed, inverse, packed, self_weights_kept, self_attended, middle, queries = call(
        self_forward,
        items,
        [timesteps],
        [
            by_item(inputs),
            by_item(chosen),
            whole(time_table),
            whole(mask_row),
            whole(first_gain_row),
            whole(first_bias_row),
            whole(self_qkv),
            later(self_out),
            later(cross_query),
        ],
        [
            rows_out(items, length, width),
            rows_out(items, length, 1),
            rows_out(items, length, 3 * width),
            rows_out(items, HEADS // 2, length, 2 * length),
            rows_out(items, length, width),
            rows_out(items, length, width),
            rows_out(items, length, width),
        ],
        [
            split_scratch(width, 3 * width),
            split_scratch(width, width),
            split_scratch(width, width),
            landing(width, width),
            landing(width, width),
            copies(2),
        ],
        6 * 6 * mac,
        "self_forward",
    )
    memory_both, pairs, cross_weights_kept, cross_attended, after = call(
        cross_forward,
        items,
        [place],
        [
            (memory, own_spec(memory.shape, items)),
            by_item(memory_far),
            by_item(queries),
            by_item(middle),
            whole(cross_kv),
            whole(cross_out),
        ],
        [
            rows_out(items, positions, width),
            rows_out(items, positions, 2 * width),
            rows_out(items, HEADS // 2, length, 2 * positions),
            rows_out(items, length, width),
            rows_out(items, length, width),
        ],
        [split_scratch(width, 2 * width), split_scratch(width, width)],
        6 * 4 * mac,
        "cross_forward",
    )

    tokens = items * length
    after_flat = after.reshape(tokens, width)
    cot_flat = cotangent.reshape(tokens, width)

    parts = feed_width // width

    def part_of(j):
        return jnp.minimum(j, parts - 1)

    feed_cols = pl.BlockSpec((width, width), lambda j: (0, part_of(j)))
    token_cols = pl.BlockSpec((tokens, width), lambda j: (0, part_of(j)))
    feed_rows = pl.BlockSpec((width, width), lambda j: (part_of(j), 0))
    (
        hidden,
        grad_after,
        reduce_g,
        expand_g,
        cross_out_g,
        second_gain_g,
        second_bias_g,
    ) = call(
        feed,
        parts + 1,
        [],
        [
            whole(after_flat),
            whole(cot_flat),
            later(cross_attended.reshape(tokens, width)),
            whole(second_gain_row),
            whole(second_bias_row),
            (expand_weight, feed_cols),
            (reduce_weight, feed_rows),
        ],
        [
            (struct(tokens, feed_width), token_cols),
            whole_out(tokens, width),
            (struct(feed_width, width), feed_rows),
            (struct(width, feed_width), feed_cols),
            whole_out(width, width),
            whole_out(1, width),
            whole_out(1, width),
        ],
        [
            split_scratch(tokens, width),
            split_scratch(tokens, width),
            landing(tokens, width),
            copies(1),
        ],
        6 * 25 * mac,
        "feed",
    )
    grad_after = grad_after.reshape(items, length, width)

    def backward():
        def cross_call(queries, pairs, kept, attended, grad_after):
            return call(
                cross_backward,
                items,
                [place],
                [
                    by_item(queries),
                    by_item(pairs),
                    by_item(kept),
                    by_item(attended),
                    by_item(grad_after),
                    whole(cross_out),
                    later(cross_query),
                    later(cross_kv),
                ],
                [
                    (struct(*memory.shape), own_spec(memory.shape, items)),
                    rows_out(items, half, width),
                    rows_out(items, length, width),
                    rows_out(items, length, width),
                    rows_out(items, positions, 2 * width),
                ],
                [
                    split_scratch(width, width),
                    split_scratch(width, width),
                    split_scratch(width, 2 * width),
                    landing(width, width),
                    landing(width, 2 * width),
                    copies(2),
                ],
                6 * 6 * mac,
                "cross_backward",
            )

        own_grad, far_grad, grad_middle, grad_queries, grad_pairs = beside(
            [],
            cross_call,
            (queries, pairs, cross_weights_kept, cross_attended, grad_after),
        )

        def flat(values):
            return values.reshape(-1, values.shape[-1])

        def cross_weights_call(*arrays):
            pairs_spec = pl.BlockSpec((items * positions, width), lambda i: (0, jnp.clip(i - 1, 0, 1)))
            ins = [whole(flat(array)) for array in arrays]
            ins[3] = (ins[3][0], pairs_spec)
            for k in (2, 4, 5):
                ins[k] = later(ins[k][0])
            return call(
                cross_weights,
                4,
                [],
                ins,
                [(struct(width, 4 * width), pl.BlockSpec((width, width), lambda i: (0, i)))],
                [
                    landing(items * positions, width),
                    landing(tokens, width),
                    landing(tokens, width),
                    copies(3),
                ],
                6 * 4 * mac,
                "cross_weights",
            )

        moved = Move(far_grad, "y")
        (cross_grads,) = beside(
            [],
            cross_weights_call,
            (
                middle,
                grad_queries,
                memory_both,
                grad_pairs,
                self_attended,
                grad_middle,
            ),
        )
        crossed = Sum(cross_grads)

        def self_call(packed, kept, attended, grad_middle):
            return call(
                self_backward,
                items,
                [],
                [
                    by_item(packed),
                    by_item(kept),
                    by_item(attended),
                    by_item(grad_middle),
                    whole(self_out),
                ],
                [rows_out(items, length, 3 * width)],
                [split_scratch(width, width)],
                6 * 4 * mac,
                "self_backward",
            )

        (grad_packed,) = beside(
            [crossed, moved],
            self_call,
            (packed, self_weights_kept, self_attended, grad_middle),
        )

        def self_weights_call(normed, grad_packed):
            normed, grad_packed = flat(normed), flat(grad_packed)
            return call(
                self_weights,
                3,
                [],
                [
                    whole(normed),
                    whole(first_gain_row),
                    whole(first_bias_row),
                    (grad_packed, pl.BlockSpec((tokens, width), lambda i: (0, i))),
                ],
                [(struct(width, 3 * width), pl.BlockSpec((width, width), lambda i: (0, i)))],
                [split_scratch(tokens, width)],
                6 * 3 * mac,
                "self_weights",
            )

        (self_grads,) = beside([crossed], self_weights_call, (normed, grad_packed))
        selfed = Sum(self_grads)

        def start_call(normed, inverse, chosen, grad_packed, grad_middle):
            return call(
                start_backward,
                items,
                [timesteps],
                [
                    by_item(normed),
                    by_item(inverse),
                    by_item(chosen),
                    by_item(grad_packed),
                    by_item(grad_middle),
                    whole(first_gain_row),
                    whole(self_qkv),
                ],
                [
                    rows_out(items, length, width),
                    whole_out(steps, width),
                    whole_out(1, width),
                    whole_out(1, width),
                    whole_out(1, width),
                ],
                [split_scratch(width, 3 * width)],
                6 * 3 * mac,
                "start_backward",
            )

        input_grad, time_rows, mask_g, first_gain_g, first_bias_g = beside(
            [crossed, selfed],
            start_call,
            (normed, inverse, chosen, grad_packed, grad_middle),
        )
        vectors = [mask_g, first_gain_g, first_bias_g, second_gain_g, second_bias_g]
        small = jnp.concatenate([*vectors, time_rows])
        small = Small(jnp.pad(small, ((0, -small.shape[0] % 8), (0, 0))))

        def output_call(hidden):
            return call(
                feed_output,
                parts,
                [],
                [whole(after_flat), (hidden, token_cols), (reduce_weight, feed_rows)],
                [whole_out(tokens, width)],
                [],
                6 * 4 * mac,
                "feed_output",
            )

        beside([selfed, crossed], None, ())
        beside([selfed, crossed, small], None, ())
        beside([selfed, crossed, small], None, ())
        crossed = End(crossed.halves)
        beside([crossed, selfed, small], None, ())
        beside([selfed, crossed, small], None, ())
        selfed = End(selfed.halves)
        crossed = beside(
            [selfed, small],
            lambda *pieces: finished(pieces, [width, 2 * width, width], "finish_cross"),
            crossed.pieces,
        )
        running = [selfed, small]
        (output,) = beside([one for one in running if one.sends], output_call, (hidden,))
        output = output.reshape(items, length, width)
        while any(one.sends for one in running):
            beside([one for one in running if one.sends], None, ())
        (self_qkv_g,) = finished(selfed.pieces, [3 * width], "finish")
        memory_grad = lax.dynamic_update_slice_in_dim(
            own_grad, moved.result, (1 - src) * items, 0
        )
        small = small.total
        sums = [small[k] for k in range(5)]
        return (output, input_grad, memory_grad, small[5 : 5 + steps], *sums, *crossed, self_qkv_g)

    def nothing():
        return jax.tree.map(
            lambda out: jnp.zeros(out.shape, out.dtype), jax.eval_shape(backward)
        )

    steps = time_table.shape[0]
    reduce_g, expand_g, cross_out_g = lax.psum((reduce_g, expand_g, cross_out_g), ALL)
    (
        output,
        input_grad,
        memory_grad,
        time_g,
        mask_g,
        first_gain_g,
        first_bias_g,
        second_gain_g,
        second_bias_g,
        cross_query_g,
        cross_kv_g,
        self_out_g,
        self_qkv_g,
    ) = lax.cond(timesteps[0] >= 0, backward, nothing)
    reduce_g, expand_g, cross_out_g = copied([reduce_g, expand_g, cross_out_g], 2)
    return (
        output,
        input_grad,
        memory_grad,
        time_g,
        mask_g,
        first_gain_g,
        first_bias_g,
        self_qkv_g,
        self_out_g,
        cross_query_g,
        cross_kv_g,
        cross_out_g,
        second_gain_g,
        second_bias_g,
        expand_g,
        reduce_g,
    )


def solution(mesh):
    tokens = P(("dp", "src"), None, None)
    placed = (tokens, P("dp", "src", None), P(("dp", "src")), P(("dp", "src"), None))
    return jax.shard_map(
        shards,
        mesh=mesh,
        in_specs=placed + (P(),) * 13 + (tokens,),
        out_specs=(tokens, tokens, P("dp", "src", None)) + (P(),) * 13,
        check_vma=False,
    )
```

```python
import functools

import jax
import jax.numpy as jnp
from jax import lax
from jax.experimental import pallas as pl
from jax.experimental.pallas import tpu as pltpu
from jax.sharding import PartitionSpec as P

HEADS = 8
EPSILON = 1e-05
ALL = ("dp", "src")
f32 = jnp.float32
bf16 = jnp.bfloat16
VMEM_LIMIT = 56 * 2**20


def split(values):
    high = values.astype(bf16)
    return high, (values - high.astype(f32)).astype(bf16)


def dot(left, right, left_dim, right_dim):
    return lax.dot_general(
        left, right, (((left_dim,), (right_dim,)), ((), ())), preferred_element_type=f32
    )


def three(left, right, left_dim=1, right_dim=0):
    left_high, left_low = left
    right_high, right_low = right
    return (
        dot(left_high, right_high, left_dim, right_dim)
        + dot(left_high, right_low, left_dim, right_dim)
        + dot(left_low, right_high, left_dim, right_dim)
    )


def keep_split(ref, values):
    high, low = split(values)
    ref[0] = high
    ref[1] = low


def pair_of(ref):
    return ref[0], ref[1]


def fetch(step, pairs, sems):
    @pl.when(step == 0)
    def _():
        for k, (source, target) in enumerate(pairs):
            pltpu.make_async_copy(source, target, sems.at[k]).start()


def await_copy(source, target, sems, k):
    pltpu.make_async_copy(source, target, sems.at[k]).wait()


def upright(row):
    n = row.shape[1]
    same = lax.broadcasted_iota(jnp.int32, (n, n), 0) == lax.broadcasted_iota(jnp.int32, (n, n), 1)
    spread_row = jnp.broadcast_to(row.astype(f32), (n, n))
    return jnp.sum(jnp.where(same, spread_row, 0.0), -1, keepdims=True)


def norm(values):
    centred = values - jnp.mean(values, -1, keepdims=True)
    inverse = lax.rsqrt(jnp.mean(centred * centred, -1, keepdims=True) + EPSILON)
    return centred * inverse, inverse


def norm_back(grad_out, normed, inverse, gain):
    scaled = grad_out * gain
    return inverse * (
        scaled
        - jnp.mean(scaled, -1, keepdims=True)
        - normed * jnp.mean(scaled * normed, -1, keepdims=True)
    )


def stacked(values):
    lane = lax.broadcasted_iota(jnp.int32, values.shape, 1)
    first = lane < values.shape[1] // 2
    return split(
        jnp.concatenate([jnp.where(first, values, 0.0), jnp.where(first, 0.0, values)], 0)
    )


def scores(left, both):
    high, low = left
    both_high, both_low = both
    return dot(
        jnp.concatenate([high, low], 1), jnp.concatenate([both_high, both_high], 1), 1, 1
    ) + dot(high, both_low, 1, 1)


def spread(weights, values, dim):
    high, low = weights
    value_high, value_low = values
    both = dot(high, jnp.concatenate([value_high, value_low], 1), dim, 0)
    size = value_high.shape[1]
    return both[:, :size] + both[:, size:] + dot(low, value_high, dim, 0)


def own_lanes(values):
    n = values.shape[0] // 2
    lane = lax.broadcasted_iota(jnp.int32, (n, values.shape[1]), 1)
    return jnp.where(lane < values.shape[1] // 2, values[:n], values[n:])


def attend(queries, keys, values, weights_ref, out_ref):
    size = 2 * queries.shape[1] // HEADS
    count = keys.shape[0]
    scale = (size // 2) ** (-0.5)
    first = lax.broadcasted_iota(jnp.int32, (queries.shape[0], size), 1) < size // 2
    first_keys = lax.broadcasted_iota(jnp.int32, (count, size), 1) < size // 2
    for pair in range(HEADS // 2):
        lanes = slice(pair * size, (pair + 1) * size)
        pair_queries = queries[:, lanes] * scale
        pair_keys = split(keys[:, lanes])
        pair_values = values[:, lanes]
        total = 0.0
        for e in range(2):
            own = first if e == 0 else jnp.logical_not(first)
            own_keys = first_keys if e == 0 else jnp.logical_not(first_keys)
            score = scores(split(jnp.where(own, pair_queries, 0.0)), pair_keys)
            exponent = jnp.exp(score - jnp.max(score, -1, keepdims=True))
            weights = exponent * (1.0 / jnp.sum(exponent, -1, keepdims=True))
            weights_ref[0, pair, :, e * count : (e + 1) * count] = weights
            total = total + spread(
                split(weights), split(jnp.where(own_keys, pair_values, 0.0)), 1
            )
        out_ref[:, lanes] = total


def attend_back(queries, keys, values, weights_ref, grad, attended, put):
    size = 2 * queries.shape[1] // HEADS
    count = keys.shape[0]
    scale = (size // 2) ** (-0.5)
    first = lax.broadcasted_iota(jnp.int32, (queries.shape[0], size), 1) < size // 2
    for pair in range(HEADS // 2):
        lanes = slice(pair * size, (pair + 1) * size)
        pair_grad = grad[:, lanes]
        grad_pair = split(pair_grad)
        products = pair_grad * attended[:, lanes]
        weights = weights_ref[0, pair]
        grad_weights = scores(grad_pair, stacked(values[:, lanes]))
        parts = []
        for e in range(2):
            own = first if e == 0 else jnp.logical_not(first)
            dots = jnp.sum(jnp.where(own, products, 0.0), -1, keepdims=True)
            cols = slice(e * count, (e + 1) * count)
            parts.append(weights[:, cols] * (grad_weights[:, cols] - dots))
        grad_scores = split(jnp.concatenate(parts, 1))
        grad_queries = spread(grad_scores, stacked(keys[:, lanes]), 1)
        grad_keys = own_lanes(spread(grad_scores, split(queries[:, lanes] * scale), 0))
        grad_values = own_lanes(spread(split(weights), grad_pair, 0))
        put(lanes, grad_queries * scale, grad_keys, grad_values)


def self_forward(
    stamps,
    inputs,
    chosen,
    time_table,
    mask_vector,
    gain,
    bias,
    qkv_weight,
    out_weight,
    query_weight,
    normed_out,
    inverse_out,
    qkv_out,
    weights_out,
    attended_out,
    middle_out,
    query_out,
    qkv_split,
    out_split,
    query_split,
    out_landed,
    query_landed,
    sems,
):
    item = pl.program_id(0)
    fetch(item, [(out_weight, out_landed), (query_weight, query_landed)], sems)

    @pl.when(item == 0)
    def _():
        keep_split(qkv_split, qkv_weight[...])

    flags = upright(chosen[0])
    start = (
        inputs[0] * (1.0 - flags)
        + flags * mask_vector[...]
        + time_table[pl.ds(stamps[item], 1), :]
    )
    normed, inverse = norm(start)
    normed_out[0] = normed
    inverse_out[0] = inverse
    packed = three(split(normed * gain[...] + bias[...]), pair_of(qkv_split))
    qkv_out[0] = packed
    width = start.shape[1]
    attend(
        packed[:, :width],
        packed[:, width : 2 * width],
        packed[:, 2 * width :],
        weights_out,
        attended_out.at[0],
    )

    @pl.when(item == 0)
    def _():
        await_copy(out_weight, out_landed, sems, 0)
        keep_split(out_split, out_landed[...])
        await_copy(query_weight, query_landed, sems, 1)
        keep_split(query_split, query_landed[...])

    middle = start + three(split(attended_out[0]), pair_of(out_split))
    middle_out[0] = middle
    query_out[0] = three(split(middle), pair_of(query_split))


def cross_forward(
    place,
    memory_own,
    memory_far,
    queries,
    middle,
    kv_weight,
    out_weight,
    memory_out,
    kv_out,
    weights_out,
    attended_out,
    after_out,
    kv_split,
    out_split,
):
    @pl.when(pl.program_id(0) == 0)
    def _():
        keep_split(kv_split, kv_weight[...])
        keep_split(out_split, out_weight[...])

    memory = jnp.concatenate([memory_own[0], memory_far[0]], 0)
    memory_out[0] = memory
    pairs = three(split(memory), pair_of(kv_split))
    kv_out[0] = pairs
    width = memory.shape[1]
    attend(queries[0], pairs[:, :width], pairs[:, width:], weights_out, attended_out.at[0])
    after_out[0] = middle[0] + three(split(attended_out[0]), pair_of(out_split))


def feed(
    after,
    cotangent,
    attended,
    gain,
    bias,
    expand,
    reduce,
    hidden_out,
    grad_after,
    reduce_grad,
    expand_grad,
    out_grad,
    gain_grad,
    bias_grad,
    normed_split,
    cot_split,
    landed,
    sems,
):
    step = pl.program_id(0)
    last = pl.num_programs(0) - 1
    fetch(step, [(attended, landed)], sems)

    @pl.when(step == 0)
    def _():
        normed, _ = norm(after[...])
        keep_split(normed_split, normed * gain[...] + bias[...])
        keep_split(cot_split, cotangent[...])
        grad_after[...] = jnp.zeros_like(grad_after)

    @pl.when(step < last)
    def _():
        expand_pair = split(expand[...])
        reduce_pair = split(reduce[...])
        pre = three(pair_of(normed_split), expand_pair)
        grad_hidden = three(pair_of(cot_split), reduce_pair, 1, 1)
        cdf = 0.5 * (1.0 + lax.erf(pre * (0.5**0.5)))
        slope = cdf + pre * (jnp.exp(-0.5 * pre * pre) * 0.3989422804014327)
        active = pre * cdf
        hidden_out[...] = active
        hidden = split(active)
        reduce_grad[...] = three(hidden, pair_of(cot_split), 0, 0)
        grad_pre = split(grad_hidden * slope)
        expand_grad[...] = three(pair_of(normed_split), grad_pre, 0, 0)
        grad_after[...] += three(grad_pre, expand_pair, 1, 1)

    @pl.when(step == last)
    def _():
        normed, inverse = norm(after[...])
        grad = grad_after[...]
        gain_grad[...] = jnp.sum(grad * normed, 0, keepdims=True)
        bias_grad[...] = jnp.sum(grad, 0, keepdims=True)
        grad = cotangent[...] + norm_back(grad, normed, inverse, gain[...])
        grad_after[...] = grad
        await_copy(attended, landed, sems, 0)
        out_grad[...] = three(split(landed[...]), split(grad), 0, 0)


def feed_output(after, hidden, reduce, output):
    @pl.when(pl.program_id(0) == 0)
    def _():
        output[...] = after[...]

    output[...] += three(split(hidden[...]), split(reduce[...]))


def cross_backward(
    place,
    queries,
    pairs,
    weights,
    attended,
    grad_after,
    out_weight,
    query_weight,
    kv_weight,
    own_grad,
    far_grad,
    middle_grad,
    grad_queries,
    grad_pairs,
    out_split,
    query_split,
    kv_split,
    query_landed,
    kv_landed,
    sems,
):
    item = pl.program_id(0)
    fetch(item, [(query_weight, query_landed), (kv_weight, kv_landed)], sems)

    @pl.when(item == 0)
    def _():
        keep_split(out_split, out_weight[...])

    width = queries.shape[2]
    upstream = grad_after[0]
    grad = three(split(upstream), pair_of(out_split), 1, 1)

    def put(lanes, query_part, key_part, value_part):
        grad_queries[0, :, lanes] = query_part
        grad_pairs[0, :, lanes] = key_part
        grad_pairs[0, :, lanes.start + width : lanes.stop + width] = value_part

    attend_back(
        queries[0],
        pairs[0, :, :width],
        pairs[0, :, width:],
        weights,
        grad,
        attended[0],
        put,
    )

    @pl.when(item == 0)
    def _():
        await_copy(query_weight, query_landed, sems, 0)
        keep_split(query_split, query_landed[...])
        await_copy(kv_weight, kv_landed, sems, 1)
        keep_split(kv_split, kv_landed[...])

    middle_grad[0] = upstream + three(split(grad_queries[0]), pair_of(query_split), 1, 1)
    memory_grad = three(split(grad_pairs[0]), pair_of(kv_split), 1, 1)
    half = own_grad.shape[1]
    own_grad[0] = memory_grad[:half]
    far_grad[0] = memory_grad[half:]


def cross_weights(
    middle,
    grad_queries,
    memory,
    grad_pairs,
    self_attended,
    grad_middle,
    out,
    memory_landed,
    attended_landed,
    grad_landed,
    sems,
):
    step = pl.program_id(0)
    fetch(
        step,
        [
            (memory, memory_landed),
            (self_attended, attended_landed),
            (grad_middle, grad_landed),
        ],
        sems,
    )

    def product(left, right):
        out[...] = three(split(left[...]), split(right[...]), 0, 0)

    @pl.when(step == 0)
    def _():
        product(middle, grad_queries)

    @pl.when(step == 1)
    def _():
        await_copy(memory, memory_landed, sems, 0)

    @pl.when((step == 1) | (step == 2))
    def _():
        product(memory_landed, grad_pairs)

    @pl.when(step == 3)
    def _():
        await_copy(self_attended, attended_landed, sems, 1)
        await_copy(grad_middle, grad_landed, sems, 2)
        product(attended_landed, grad_landed)


def self_backward(
    packed,
    weights,
    attended,
    grad_middle,
    out_weight,
    grad_packed,
    out_split,
):
    @pl.when(pl.program_id(0) == 0)
    def _():
        keep_split(out_split, out_weight[...])

    width = attended.shape[2]
    grad = three(split(grad_middle[0]), pair_of(out_split), 1, 1)

    def put(lanes, query_part, key_part, value_part):
        for k, part in enumerate((query_part, key_part, value_part)):
            grad_packed[0, :, lanes.start + k * width : lanes.stop + k * width] = part

    attend_back(
        packed[0, :, :width],
        packed[0, :, width : 2 * width],
        packed[0, :, 2 * width :],
        weights,
        grad,
        attended[0],
        put,
    )


def self_weights(normed, gain, bias, grad_packed, out, normed_split):
    @pl.when(pl.program_id(0) == 0)
    def _():
        keep_split(normed_split, normed[...] * gain[...] + bias[...])

    out[...] = three(pair_of(normed_split), split(grad_packed[...]), 0, 0)


def start_backward(
    stamps,
    normed,
    inverse,
    chosen,
    grad_packed,
    grad_middle,
    gain,
    qkv_weight,
    input_grad,
    time_grad,
    mask_grad,
    gain_grad,
    bias_grad,
    qkv_split,
):
    item = pl.program_id(0)

    @pl.when(item == 0)
    def _():
        keep_split(qkv_split, qkv_weight[...])
        for ref in (time_grad, mask_grad, gain_grad, bias_grad):
            ref[...] = jnp.zeros_like(ref)

    grad_normed = three(split(grad_packed[0]), pair_of(qkv_split), 1, 1)
    unit = normed[0]
    gain_grad[...] += jnp.sum(grad_normed * unit, 0, keepdims=True)
    bias_grad[...] += jnp.sum(grad_normed, 0, keepdims=True)
    grad_start = grad_middle[0] + norm_back(grad_normed, unit, inverse[0], gain[...])
    flags = upright(chosen[0])
    input_grad[0] = grad_start * (1.0 - flags)
    mask_grad[...] += jnp.sum(grad_start * flags, 0, keepdims=True)
    row = pl.ds(stamps[item], 1)
    time_grad[row, :] += jnp.sum(grad_start, 0, keepdims=True)


def exchange(values, kind, offset=1):
    groups, halves = lax.axis_size("dp"), lax.axis_size("src")
    shift = {"core": offset, "x": 2 * offset, "z": 4 * offset, "y": 0}[kind]
    pairs = []
    for d in range(groups):
        for s in range(halves):
            target = d * halves + (s ^ 1) if kind == "y" else (d ^ shift) * halves + s
            pairs.append((d * halves + s, target))
    return lax.ppermute(values, ALL, pairs)


def take(values, dim, index):
    return lax.dynamic_index_in_dim(values, index, dim, keepdims=False)


def place_of():
    group = lax.axis_index("dp")
    return group & 1, (group >> 1) & 1, lax.axis_index("src"), (group >> 2) & 3


def doubled(values, received, bit):
    return jnp.where(
        bit == 0, jnp.concatenate([values, received]), jnp.concatenate([received, values])
    )


class Sum:
    def __init__(self, values):
        self.steps = self.run(values)
        self.sends = next(self.steps)

    def run(self, values):
        core, x, y, z = place_of()
        rows, width = values.shape
        values = values.reshape(2, rows // 2, width)
        (received,) = yield [(take(values, 0, 1 - core), "core", 1)]
        values = take(values, 0, core) + received
        values = values.reshape(2, 2, 2, 4, rows // 64, width)
        one, two = values[0], values[1]
        for first, second, bit, other in (("x", "y", x, y), ("y", "x", y, x)):
            got_one, got_two = yield [
                (take(one, 0, 1 - bit), first, 1),
                (take(two, 0, 1 - other), second, 1),
            ]
            one = take(one, 0, bit) + got_one
            two = take(two, 0, other) + got_two
        both = jnp.stack([one, two])
        got = yield [(take(both, 1, z ^ k), "z", k) for k in (1, 2, 3)]
        share = take(both, 1, z) + got[0] + got[1] + got[2]
        offset = 4
        while 4 * offset < lax.axis_size("dp"):
            share = share + exchange(share, "z", offset)
            offset *= 2
        got = yield [(share, "z", k) for k in (1, 2, 3)]
        parts = [share, *got]

        def at(k):
            found = parts[0]
            for j in (1, 2, 3):
                found = jnp.where((z ^ j) == k, parts[j], found)
            return found

        both = jnp.stack([at(k) for k in range(4)], 1)
        one, two = both[0].reshape(rows // 16, width), both[1].reshape(rows // 16, width)
        got_one, got_two = yield [(one, "y", 1), (two, "x", 1)]
        self.halves = (doubled(one, got_one, y), doubled(two, got_two, x))
        yield []

    def put(self, received):
        self.sends = self.steps.send(received)


class End(Sum):
    def __init__(self, halves):
        self.steps = self.finish(*halves)
        self.sends = next(self.steps)

    def finish(self, one, two):
        _, x, y, _ = place_of()
        got_one, got_two = yield [(one, "x", 1), (two, "y", 1)]
        mine = jnp.concatenate([doubled(one, got_one, x), doubled(two, got_two, y)])
        (received,) = yield [(mine, "core", 1)]
        self.pieces = (mine, received)
        yield []


class Move:
    def __init__(self, values, kind):
        self.sends = [(values, kind, 1)]

    def put(self, received):
        (self.result,) = received
        self.sends = []


class Small:
    def __init__(self, values):
        self.steps = self.run(values)
        self.sends = next(self.steps)

    def run(self, values):
        kinds, offset = [("core", 1), ("x", 1), ("y", 1)], 1
        while 4 * offset < lax.axis_size("dp"):
            kinds.append(("z", offset))
            offset *= 2
        for kind, offset in kinds:
            (received,) = yield [(values, kind, offset)]
            values = values + received
        self.total = values
        yield []

    def put(self, received):
        self.sends = self.steps.send(received)


def beside(sums, kernel, arrays):
    sent = [[array for array, _, _ in one.sends] for one in sums]
    ways = [[(kind, offset) for _, kind, offset in one.sends] for one in sums]
    sent, arrays = lax.optimization_barrier((sent, arrays))
    got = [
        [exchange(array, *way) for array, way in zip(*each)] for each in zip(sent, ways)
    ]
    outs = kernel(*arrays) if kernel else ()
    outs, got = lax.optimization_barrier((outs, got))
    for one, received in zip(sums, got):
        one.put(received)
    return outs


def finish(place, mine, far, *outs):
    start = 0
    for out in outs:
        cols = slice(start, start + out.shape[1])
        start += out.shape[1]

        @pl.when(pl.program_id(0) == 0)
        def _(out=out, cols=cols):
            out[...] = mine[:, cols]

        @pl.when(pl.program_id(0) == 1)
        def _(out=out, cols=cols):
            out[...] = far[:, cols]


def finished(pieces, widths, name):
    rows = pieces[0].shape[0]
    place = place_of()[0].astype(jnp.int32).reshape(1)
    return call(
        finish,
        2,
        [place],
        [whole(piece) for piece in pieces],
        [
            (struct(2 * rows, w), pl.BlockSpec((rows, w), lambda i, place: (place[0] ^ i, 0)))
            for w in widths
        ],
        [],
        0,
        name,
    )


def copy_out(*refs):
    count = len(refs) // 2
    for source, target in zip(refs[:count], refs[count:]):
        target[...] = source[...]


def copied(arrays, steps):
    blocks = [
        pl.BlockSpec((array.shape[0] // steps, array.shape[1]), lambda i: (i, 0))
        for array in arrays
    ]
    return call(
        copy_out,
        steps,
        [],
        list(zip(arrays, blocks)),
        [(struct(*array.shape), block) for array, block in zip(arrays, blocks)],
        [],
        0,
        "copied",
    )


def whole_spec(shape):
    return pl.BlockSpec(shape, lambda i, *_: (0,) * len(shape))


def item_spec(shape):
    return pl.BlockSpec((1,) + shape[1:], lambda i, *_: (i,) + (0,) * (len(shape) - 1))


def own_spec(shape, items):
    return pl.BlockSpec((1,) + shape[1:], lambda i, place: (place[0] * items + i, 0, 0))


def struct(*shape):
    return jax.ShapeDtypeStruct(shape, f32)


def call(kernel, grid, prefetch, ins, outs, scratch, flops, name):
    built = pl.pallas_call(
        kernel,
        grid_spec=pltpu.PrefetchScalarGridSpec(
            num_scalar_prefetch=len(prefetch),
            grid=(grid,),
            in_specs=[spec for _, spec in ins],
            out_specs=[spec for _, spec in outs],
            scratch_shapes=scratch,
        ),
        out_shape=[out for out, _ in outs],
        compiler_params=pltpu.CompilerParams(
            dimension_semantics=("arbitrary",), vmem_limit_bytes=VMEM_LIMIT
        ),
        cost_estimate=pl.CostEstimate(flops=flops, bytes_accessed=0, transcendentals=0),
        name=name,
    )
    return built(*prefetch, *[array for array, _ in ins])


def split_scratch(*shape):
    return pltpu.VMEM((2,) + shape, bf16)


def whole(array):
    return (array, whole_spec(array.shape))


def later(array):
    return (array, pl.BlockSpec(memory_space=pl.ANY))


def landing(*shape):
    return pltpu.VMEM(shape, f32)


def copies(count):
    return pltpu.SemaphoreType.DMA((count,))


def by_item(array):
    return (array, item_spec(array.shape))


def shards(
    inputs,
    memory,
    timesteps,
    mask_flags,
    time_table,
    mask_vector,
    first_gain,
    first_bias,
    self_qkv,
    self_out,
    cross_query,
    cross_kv,
    cross_out,
    second_gain,
    second_bias,
    expand_weight,
    reduce_weight,
    cotangent,
):
    items, length, width = inputs.shape
    half = memory.shape[1]
    positions = 2 * half
    feed_width = expand_weight.shape[1]
    mac = items * length * width * width
    swap = [(0, 1), (1, 0)]
    src = lax.axis_index("src")
    place = src.astype(jnp.int32).reshape(1)

    memory_far = lax.ppermute(
        lax.dynamic_slice_in_dim(memory, (1 - src) * items, items, 0), "src", swap
    )
    chosen = mask_flags[:, None, :]
    vectors = [v[None, :] for v in (mask_vector, first_gain, first_bias, second_gain, second_bias)]
    mask_row, first_gain_row, first_bias_row, second_gain_row, second_bias_row = vectors

    def rows_out(*shape):
        return (struct(*shape), item_spec(shape))

    def whole_out(*shape):
        return (struct(*shape), whole_spec(shape))

    normed, inverse, packed, self_weights_kept, self_attended, middle, queries = call(
        self_forward,
        items,
        [timesteps],
        [
            by_item(inputs),
            by_item(chosen),
            whole(time_table),
            whole(mask_row),
            whole(first_gain_row),
            whole(first_bias_row),
            whole(self_qkv),
            later(self_out),
            later(cross_query),
        ],
        [
            rows_out(items, length, width),
            rows_out(items, length, 1),
            rows_out(items, length, 3 * width),
            rows_out(items, HEADS // 2, length, 2 * length),
            rows_out(items, length, width),
            rows_out(items, length, width),
            rows_out(items, length, width),
        ],
        [
            split_scratch(width, 3 * width),
            split_scratch(width, width),
            split_scratch(width, width),
            landing(width, width),
            landing(width, width),
            copies(2),
        ],
        6 * 6 * mac,
        "self_forward",
    )
    memory_both, pairs, cross_weights_kept, cross_attended, after = call(
        cross_forward,
        items,
        [place],
        [
            (memory, own_spec(memory.shape, items)),
            by_item(memory_far),
            by_item(queries),
            by_item(middle),
            whole(cross_kv),
            whole(cross_out),
        ],
        [
            rows_out(items, positions, width),
            rows_out(items, positions, 2 * width),
            rows_out(items, HEADS // 2, length, 2 * positions),
            rows_out(items, length, width),
            rows_out(items, length, width),
        ],
        [split_scratch(width, 2 * width), split_scratch(width, width)],
        6 * 4 * mac,
        "cross_forward",
    )

    tokens = items * length
    after_flat = after.reshape(tokens, width)
    cot_flat = cotangent.reshape(tokens, width)

    parts = feed_width // width

    def part_of(j):
        return jnp.minimum(j, parts - 1)

    feed_cols = pl.BlockSpec((width, width), lambda j: (0, part_of(j)))
    token_cols = pl.BlockSpec((tokens, width), lambda j: (0, part_of(j)))
    feed_rows = pl.BlockSpec((width, width), lambda j: (part_of(j), 0))
    (
        hidden,
        grad_after,
        reduce_g,
        expand_g,
        cross_out_g,
        second_gain_g,
        second_bias_g,
    ) = call(
        feed,
        parts + 1,
        [],
        [
            whole(after_flat),
            whole(cot_flat),
            later(cross_attended.reshape(tokens, width)),
            whole(second_gain_row),
            whole(second_bias_row),
            (expand_weight, feed_cols),
            (reduce_weight, feed_rows),
        ],
        [
            (struct(tokens, feed_width), token_cols),
            whole_out(tokens, width),
            (struct(feed_width, width), feed_rows),
            (struct(width, feed_width), feed_cols),
            whole_out(width, width),
            whole_out(1, width),
            whole_out(1, width),
        ],
        [
            split_scratch(tokens, width),
            split_scratch(tokens, width),
            landing(tokens, width),
            copies(1),
        ],
        6 * 25 * mac,
        "feed",
    )
    grad_after = grad_after.reshape(items, length, width)

    def backward():
        def cross_call(queries, pairs, kept, attended, grad_after):
            return call(
                cross_backward,
                items,
                [place],
                [
                    by_item(queries),
                    by_item(pairs),
                    by_item(kept),
                    by_item(attended),
                    by_item(grad_after),
                    whole(cross_out),
                    later(cross_query),
                    later(cross_kv),
                ],
                [
                    (struct(*memory.shape), own_spec(memory.shape, items)),
                    rows_out(items, half, width),
                    rows_out(items, length, width),
                    rows_out(items, length, width),
                    rows_out(items, positions, 2 * width),
                ],
                [
                    split_scratch(width, width),
                    split_scratch(width, width),
                    split_scratch(width, 2 * width),
                    landing(width, width),
                    landing(width, 2 * width),
                    copies(2),
                ],
                6 * 6 * mac,
                "cross_backward",
            )

        own_grad, far_grad, grad_middle, grad_queries, grad_pairs = beside(
            [],
            cross_call,
            (queries, pairs, cross_weights_kept, cross_attended, grad_after),
        )

        def flat(values):
            return values.reshape(-1, values.shape[-1])

        def cross_weights_call(*arrays):
            pairs_spec = pl.BlockSpec((items * positions, width), lambda i: (0, jnp.clip(i - 1, 0, 1)))
            ins = [whole(flat(array)) for array in arrays]
            ins[3] = (ins[3][0], pairs_spec)
            for k in (2, 4, 5):
                ins[k] = later(ins[k][0])
            return call(
                cross_weights,
                4,
                [],
                ins,
                [(struct(width, 4 * width), pl.BlockSpec((width, width), lambda i: (0, i)))],
                [
                    landing(items * positions, width),
                    landing(tokens, width),
                    landing(tokens, width),
                    copies(3),
                ],
                6 * 4 * mac,
                "cross_weights",
            )

        moved = Move(far_grad, "y")
        (cross_grads,) = beside(
            [],
            cross_weights_call,
            (
                middle,
                grad_queries,
                memory_both,
                grad_pairs,
                self_attended,
                grad_middle,
            ),
        )
        crossed = Sum(cross_grads)

        def self_call(packed, kept, attended, grad_middle):
            return call(
                self_backward,
                items,
                [],
                [
                    by_item(packed),
                    by_item(kept),
                    by_item(attended),
                    by_item(grad_middle),
                    whole(self_out),
                ],
                [rows_out(items, length, 3 * width)],
                [split_scratch(width, width)],
                6 * 4 * mac,
                "self_backward",
            )

        (grad_packed,) = beside(
            [crossed, moved],
            self_call,
            (packed, self_weights_kept, self_attended, grad_middle),
        )

        def self_weights_call(normed, grad_packed):
            normed, grad_packed = flat(normed), flat(grad_packed)
            return call(
                self_weights,
                3,
                [],
                [
                    whole(normed),
                    whole(first_gain_row),
                    whole(first_bias_row),
                    (grad_packed, pl.BlockSpec((tokens, width), lambda i: (0, i))),
                ],
                [(struct(width, 3 * width), pl.BlockSpec((width, width), lambda i: (0, i)))],
                [split_scratch(tokens, width)],
                6 * 3 * mac,
                "self_weights",
            )

        (self_grads,) = beside([crossed], self_weights_call, (normed, grad_packed))
        selfed = Sum(self_grads)

        def start_call(normed, inverse, chosen, grad_packed, grad_middle):
            return call(
                start_backward,
                items,
                [timesteps],
                [
                    by_item(normed),
                    by_item(inverse),
                    by_item(chosen),
                    by_item(grad_packed),
                    by_item(grad_middle),
                    whole(first_gain_row),
                    whole(self_qkv),
                ],
                [
                    rows_out(items, length, width),
                    whole_out(steps, width),
                    whole_out(1, width),
                    whole_out(1, width),
                    whole_out(1, width),
                ],
                [split_scratch(width, 3 * width)],
                6 * 3 * mac,
                "start_backward",
            )

        input_grad, time_rows, mask_g, first_gain_g, first_bias_g = beside(
            [crossed, selfed],
            start_call,
            (normed, inverse, chosen, grad_packed, grad_middle),
        )
        vectors = [mask_g, first_gain_g, first_bias_g, second_gain_g, second_bias_g]
        small = jnp.concatenate([*vectors, time_rows])
        small = Small(jnp.pad(small, ((0, -small.shape[0] % 8), (0, 0))))

        def output_call(hidden):
            return call(
                feed_output,
                parts,
                [],
                [whole(after_flat), (hidden, token_cols), (reduce_weight, feed_rows)],
                [whole_out(tokens, width)],
                [],
                6 * 4 * mac,
                "feed_output",
            )

        beside([selfed, crossed], None, ())
        beside([selfed, crossed, small], None, ())
        beside([selfed, crossed, small], None, ())
        crossed = End(crossed.halves)
        beside([crossed, selfed, small], None, ())
        beside([selfed, crossed, small], None, ())
        selfed = End(selfed.halves)
        (output,) = beside([selfed, small], output_call, (hidden,))
        output = output.reshape(items, length, width)
        crossed = beside(
            [selfed, small] if small.sends else [selfed],
            lambda *pieces: finished(pieces, [width, 2 * width, width], "finish_cross"),
            crossed.pieces,
        )
        while small.sends:
            beside([small], None, ())
        (self_qkv_g,) = finished(selfed.pieces, [3 * width], "finish")
        memory_grad = lax.dynamic_update_slice_in_dim(
            own_grad, moved.result, (1 - src) * items, 0
        )
        small = small.total
        sums = [small[k] for k in range(5)]
        return (output, input_grad, memory_grad, small[5 : 5 + steps], *sums, *crossed, self_qkv_g)

    def nothing():
        return jax.tree.map(
            lambda out: jnp.zeros(out.shape, out.dtype), jax.eval_shape(backward)
        )

    steps = time_table.shape[0]
    reduce_g, expand_g, cross_out_g = lax.psum((reduce_g, expand_g, cross_out_g), ALL)
    (
        output,
        input_grad,
        memory_grad,
        time_g,
        mask_g,
        first_gain_g,
        first_bias_g,
        second_gain_g,
        second_bias_g,
        cross_query_g,
        cross_kv_g,
        self_out_g,
        self_qkv_g,
    ) = lax.cond(timesteps[0] >= 0, backward, nothing)
    reduce_g, expand_g, cross_out_g = copied([reduce_g, expand_g, cross_out_g], 2)
    return (
        output,
        input_grad,
        memory_grad,
        time_g,
        mask_g,
        first_gain_g,
        first_bias_g,
        self_qkv_g,
        self_out_g,
        cross_query_g,
        cross_kv_g,
        cross_out_g,
        second_gain_g,
        second_bias_g,
        expand_g,
        reduce_g,
    )


def solution(mesh):
    tokens = P(("dp", "src"), None, None)
    placed = (tokens, P("dp", "src", None), P(("dp", "src")), P(("dp", "src"), None))
    return jax.shard_map(
        shards,
        mesh=mesh,
        in_specs=placed + (P(),) * 13 + (tokens,),
        out_specs=(tokens, tokens, P("dp", "src", None)) + (P(),) * 13,
        check_vma=False,
    )
```
